256 devices in a mesh: grp: 16 (over x, y), chan: 16 (over z, core).
Axes of the slice: x: 4, y: 4, z: 8, core: 2. Of those that a mesh axis runs over, the one named last changes fastest.
Arguments:
- visibilities: float32 [2, 1536, 32768], P(None, 'chan', 'grp'), may hold values from -7 to 7
- baseline_antennas: int32 [2, 32768], P(None, 'grp'), may hold values from 0 to 349, as said below
- group_ids: int32 [16, 2048], P('grp'), may hold values from 0 to 127, as said below
- sky_model: float32 [2, 1536, 2048], P(None, 'chan', 'grp'), may hold values from -4 to 4
- starting_gain_values: float32 [2, 1536, 350], P(None, 'chan'), may hold values from 0.6 to 1.4
- antenna_coordinates: float32 [2, 350], replicated, may hold values from -1 to 1
Outputs:
- gains: float32 [2, 1536, 350], P(None, 'chan')
- calibrated: float32 [2, 1536, 2048], P(None, 'chan', 'grp')
- chi_square: float32 [1536], P('chan')
The draws below stay inside these ranges and needn't reach their ends.
Inputs may be any that keep to these rules, and one draw needn't show every extreme that they name: `baseline_antennas`: the two antennas of a baseline differ. `group_ids`: each row holds the baselines of one index of grp; ids never fall along a row, start at 0, and each of the 128 ids names one or more baselines.
All inputs are finite; a program needn't handle non-finite values.
Results may differ from the reference program's by a relative error of at most 0.0001.
Values sent between devices are 32-bit elements; how exact they have to be, the bound alone decides.
A program may use at most 256 MiB of HBM per device.

```python
import jax
import jax.numpy as jnp
from jax import lax

ANTENNA_COUNT = 350
CHANNEL_COUNT = 1536
NDLY = 64
ITERS = 4
BL_DEV = 2048
GRP_DEV = 128
BASELINE_COUNT = 32768
REDUNDANT_COUNT = 2048
N_GRP = 16


def draw_scene(key):
    random_subkeys = jax.random.split(key, 8)
    antenna_locations = jax.random.uniform(random_subkeys[0], (2, ANTENNA_COUNT), jnp.float32, -1.0, 1.0)
    leading_antenna = jax.random.randint(random_subkeys[1], (BASELINE_COUNT,), 0, ANTENNA_COUNT, dtype=jnp.int32)
    index_shift = jax.random.randint(random_subkeys[2], (BASELINE_COUNT,), 1, ANTENNA_COUNT, dtype=jnp.int32)
    pair_table = jnp.stack([leading_antenna, (leading_antenna + index_shift) % ANTENNA_COUNT]).astype(jnp.int32)
    row_keys = jax.random.split(random_subkeys[3], N_GRP)
    starts = jax.vmap(lambda row_key: jax.random.permutation(row_key, BL_DEV - 1)[:GRP_DEV - 1] + 1)(row_keys)
    places = jnp.arange(BL_DEV, dtype=jnp.int32)
    group_random_key = jnp.sum((starts[:, None, :] <= places[None, :, None]).astype(jnp.int32), axis=2).astype(jnp.int32)
    global_group_index = (group_random_key + GRP_DEV * jnp.arange(N_GRP, dtype=jnp.int32)[:, None]).reshape(-1)
    residual_value = antenna_locations[:, pair_table[0]] - antenna_locations[:, pair_table[1]]
    group_members = jax.ops.segment_sum(jnp.ones((BASELINE_COUNT,), jnp.float32), global_group_index, num_segments=REDUNDANT_COUNT)
    vectors = jax.ops.segment_sum(residual_value.T, global_group_index, num_segments=REDUNDANT_COUNT).T / group_members[None, :]
    sky_random_key = jnp.clip(jax.random.normal(random_subkeys[4], (2, CHANNEL_COUNT, REDUNDANT_COUNT), jnp.float32), -4.0, 4.0)
    slope_draw = jax.random.uniform(random_subkeys[5], (2,), jnp.float32, -2.0, 2.0)
    tilt_draw = jax.random.uniform(random_subkeys[6], (2, CHANNEL_COUNT), jnp.float32, -0.5, 0.5)
    frequency = 1.0 + jnp.arange(CHANNEL_COUNT, dtype=jnp.float32) / CHANNEL_COUNT
    along_slope = slope_draw[0] * vectors[0] + slope_draw[1] * vectors[1]
    phase_turn = frequency[:, None] * along_slope[None, :] + tilt_draw[0][:, None] * vectors[0][None, :] + tilt_draw[1][:, None] * vectors[1][None, :]
    rotation_cos = jnp.cos(phase_turn)
    rotation_sin = jnp.sin(phase_turn)
    rotated = jnp.stack([sky_random_key[0] * rotation_cos - sky_random_key[1] * rotation_sin, sky_random_key[0] * rotation_sin + sky_random_key[1] * rotation_cos])
    noise_draw = jnp.clip(jax.random.normal(random_subkeys[7], (2, CHANNEL_COUNT, BASELINE_COUNT), jnp.float32), -4.0, 4.0)
    observed_visibility = rotated[:, :, global_group_index] + 0.3 * noise_draw
    return (antenna_locations, pair_table, group_random_key, sky_random_key, observed_visibility)


def draw_visibilities(key, part):
    scene_parts = draw_scene(key)
    return scene_parts[4]


def draw_baseline_antennas(key, part):
    scene_parts = draw_scene(key)
    return scene_parts[1]


def draw_group_ids(key, part):
    scene_parts = draw_scene(key)
    return scene_parts[2]


def draw_sky_model(key, part):
    scene_parts = draw_scene(key)
    return scene_parts[3]


def draw_antenna_coordinates(key, part):
    scene_parts = draw_scene(key)
    return scene_parts[0]


def level_of(stream_key, shape, cuts, least, high):
    def one(dim, blocks):
        heights = jax.random.uniform(jax.random.fold_in(jax.random.fold_in(stream_key, 6), dim), (blocks,), jnp.float32, least / len(cuts), high / len(cuts))
        return jnp.repeat(jnp.exp(heights), shape[dim] // blocks).reshape((-1,) + (1,) * (len(shape) - dim - 1))

    level = one(*cuts[0])
    for cut in cuts[1:]:
        level = level * one(*cut)
    return level


def setup_inputs(seed: int = 0) -> dict:
    key_list = jax.random.split(jax.random.key(seed), 7)
    return {
        "visibilities": draw_visibilities(jax.random.fold_in(key_list[6], 71), 0),
        "baseline_antennas": draw_baseline_antennas(jax.random.fold_in(key_list[6], 71), 0),
        "group_ids": draw_group_ids(jax.random.fold_in(key_list[6], 71), 0),
        "sky_model": draw_sky_model(jax.random.fold_in(key_list[6], 71), 0),
        "starting_gain_values": jnp.clip(0.6 + 0.79999995 * jax.random.uniform(key_list[4], (2, CHANNEL_COUNT, ANTENNA_COUNT), jnp.float32) ** level_of(key_list[4], (2, CHANNEL_COUNT, ANTENNA_COUNT), ((1, 16),), -0.2, 0.2), 0.6, 1.4),
        "antenna_coordinates": draw_antenna_coordinates(jax.random.fold_in(key_list[6], 71), 0),
    }


highest = lax.Precision.HIGHEST
ridge_term = 0.5
epsilon = 1e-06

def conjugated_value(number):
    return jnp.stack([number[0], -number[1]])

def complex_product(former, latter):
    return jnp.stack([former[0] * latter[0] - former[1] * latter[1], former[0] * latter[1] + former[1] * latter[0]])

def absolute_size(number):
    return number[0] * number[0] + number[1] * number[1]

def segment_final_index(source, indices, number):
    summed = jax.ops.segment_sum(jnp.moveaxis(source, -1, 0), indices, num_segments=number)
    return jnp.moveaxis(summed, 0, -1)

def delay_tables(first_channel, number, band_size, mode_count):
    channel_ids = first_channel + jnp.arange(number, dtype=jnp.int32)
    turn_counts = channel_ids[:, None] * (jnp.arange(mode_count, dtype=jnp.int32)[None, :] - mode_count // 2) % band_size
    angles = 2.0 * jnp.pi / band_size * turn_counts.astype(jnp.float32)
    frequency = 1.0 + channel_ids.astype(jnp.float32) / band_size
    return (jnp.cos(angles), jnp.sin(angles), frequency)

def delay_coefficients(cross_ratio, cosines, sine_table):
    real_part = (jnp.einsum('fk,fj->jk', cross_ratio[0], cosines, precision=highest) + jnp.einsum('fk,fj->jk', cross_ratio[1], sine_table, precision=highest)) / CHANNEL_COUNT
    imag_part = (jnp.einsum('fk,fj->jk', cross_ratio[1], cosines, precision=highest) - jnp.einsum('fk,fj->jk', cross_ratio[0], sine_table, precision=highest)) / CHANNEL_COUNT
    return (real_part, imag_part)

def smooth_phase(real_part, imag_part, cosines, sine_table):
    return jnp.einsum('jk,fj->fk', imag_part, cosines, precision=highest) + jnp.einsum('jk,fj->fk', real_part, sine_table, precision=highest)

def channel_sums(unique, sky_part, phases, vectors):
    model_power = absolute_size(sky_part)
    squared = model_power * model_power
    east_part = vectors[0][None, :]
    north_part = vectors[1][None, :]
    return jnp.stack([lax.optimization_barrier(jnp.sum(absolute_size(unique), axis=1)), lax.optimization_barrier(jnp.sum(model_power, axis=1)), lax.optimization_barrier(jnp.sum(squared * east_part * east_part, axis=1)), lax.optimization_barrier(jnp.sum(squared * east_part * north_part, axis=1)), lax.optimization_barrier(jnp.sum(squared * north_part * north_part, axis=1)), lax.optimization_barrier(jnp.sum(model_power * phases * east_part, axis=1)), lax.optimization_barrier(jnp.sum(model_power * phases * north_part, axis=1))])

def solve_pair(entry_xx, entry_xy, entry_yy, right_x, right_y):
    ridge_shift = 0.001 * (entry_xx + entry_yy) + epsilon
    diag_first = entry_xx + ridge_shift
    diag_second = entry_yy + ridge_shift
    determinant = diag_first * diag_second - entry_xy * entry_xy
    return ((diag_second * right_x - entry_xy * right_y) / determinant, (diag_first * right_y - entry_xy * right_x) / determinant)

def slope_terms(totals, frequency):
    squared = frequency * frequency
    return jnp.stack([jnp.sum(squared * totals[2]), jnp.sum(squared * totals[3]), jnp.sum(squared * totals[4]), jnp.sum(frequency * totals[5]), jnp.sum(frequency * totals[6])])

def slope_fit(terms):
    east_part, north_part = solve_pair(terms[0], terms[1], terms[2], terms[3], terms[4])
    return jnp.stack([east_part, north_part])

def apply_fit(unique, totals, frequency, delay_slope, vectors):
    amplitude = jnp.sqrt((totals[0] + epsilon) / (totals[1] + epsilon))
    tilt_east, tilt_north = solve_pair(totals[2], totals[3], totals[4], totals[5], totals[6])
    tilt_east = tilt_east - frequency * delay_slope[0]
    tilt_north = tilt_north - frequency * delay_slope[1]
    along_slope = delay_slope[0] * vectors[0] + delay_slope[1] * vectors[1]
    phase_turn = frequency[:, None] * along_slope[None, :] + tilt_east[:, None] * vectors[0][None, :] + tilt_north[:, None] * vectors[1][None, :]
    rotation_cos = jnp.cos(phase_turn)
    rotation_sin = jnp.sin(phase_turn)
    scale_back = 1.0 / amplitude[:, None]
    return jnp.stack([(unique[0] * rotation_cos + unique[1] * rotation_sin) * scale_back, (unique[1] * rotation_cos - unique[0] * rotation_sin) * scale_back])

def reference(visibilities, baseline_antennas, group_ids, sky_model, starting_gain_values, antenna_coordinates):
    global_group_index = (group_ids + GRP_DEV * jnp.arange(N_GRP, dtype=jnp.int32)[:, None]).reshape(-1).astype(jnp.int32)
    leading_antenna = baseline_antennas[0]
    trailing_antenna = baseline_antennas[1]

    def unique_fit(current_gain):
        leading_gain = current_gain[:, :, leading_antenna]
        trailing_gain = current_gain[:, :, trailing_antenna]
        weights = complex_product(leading_gain, conjugated_value(trailing_gain))
        update_numerator = segment_final_index(complex_product(visibilities, conjugated_value(weights)), global_group_index, REDUNDANT_COUNT)
        update_denominator = segment_final_index(absolute_size(weights), global_group_index, REDUNDANT_COUNT) + ridge_term
        return (update_numerator / update_denominator[None], weights, leading_gain, trailing_gain)
    current_gain = starting_gain_values
    for iteration in range(ITERS):
        unique, weights, leading_gain, trailing_gain = unique_fit(current_gain)
        unique_rows = unique[:, :, global_group_index]
        first_axis_share = complex_product(conjugated_value(trailing_gain), unique_rows)
        second_axis_share = complex_product(leading_gain, unique_rows)
        update_numerator = segment_final_index(complex_product(conjugated_value(first_axis_share), visibilities), leading_antenna, ANTENNA_COUNT) + segment_final_index(complex_product(second_axis_share, conjugated_value(visibilities)), trailing_antenna, ANTENNA_COUNT)
        update_denominator = segment_final_index(absolute_size(first_axis_share), leading_antenna, ANTENNA_COUNT) + segment_final_index(absolute_size(second_axis_share), trailing_antenna, ANTENNA_COUNT)
        current_gain = 0.5 * current_gain + 0.5 * update_numerator / (update_denominator[None] + ridge_term)
    unique, weights, leading_gain, trailing_gain = unique_fit(current_gain)
    misfit = visibilities - complex_product(weights, unique[:, :, global_group_index])
    chi_square = lax.optimization_barrier(jnp.sum(absolute_size(misfit), axis=1))
    residual_value = antenna_coordinates[:, leading_antenna] - antenna_coordinates[:, trailing_antenna]
    group_members = jax.ops.segment_sum(jnp.ones(leading_antenna.shape, jnp.float32), global_group_index, num_segments=REDUNDANT_COUNT)
    vectors = segment_final_index(residual_value, global_group_index, REDUNDANT_COUNT) / group_members[None, :]
    cosines, sine_table, frequency = delay_tables(0, CHANNEL_COUNT, CHANNEL_COUNT, NDLY)
    cross_ratio = complex_product(unique, conjugated_value(sky_model))
    real_part, imag_part = delay_coefficients(cross_ratio, cosines, sine_table)
    phases = smooth_phase(real_part, imag_part, cosines, sine_table)
    totals = channel_sums(unique, sky_model, phases, vectors)
    delay_slope = slope_fit(slope_terms(totals, frequency))
    calibrated = apply_fit(unique, totals, frequency, delay_slope, vectors)
    return (current_gain, calibrated, chi_square)
```

```python
import functools

import jax
import jax.numpy as jnp
import numpy as np
from jax import lax
from jax.experimental import pallas as pl
from jax.experimental.pallas import tpu as pltpu
from jax.sharding import PartitionSpec as P

CHANNEL_COUNT = 1536
NDLY = 64
ITERS = 4
RIDGE = 0.5
EPSILON = 1e-06

N = 16
ANT = 350
ANT_PAD = 384
CH = 96
BL = 2048
GRP = 128
TILE = 256
STEPS = BL // TILE
ROWS = 8
OWNERS = CH // ROWS

MESH = pl.DeviceIdType.MESH
HIGHEST = lax.Precision.HIGHEST
f32 = jnp.float32
bf16 = jnp.bfloat16


def owner_of(block):
    return block + 1 + block // 4


def two_parts(number):
    first = number.astype(bf16)
    return first, (number - first.astype(f32)).astype(bf16)


def dot(left, right):
    return jnp.dot(left, right, preferred_element_type=f32)


def dot_last(left, right):
    return lax.dot_general(left, right, (((1,), (1,)), ((), ())), preferred_element_type=f32)


def solve_pair(entry_xx, entry_xy, entry_yy, right_x, right_y):
    ridge_shift = 0.001 * (entry_xx + entry_yy) + EPSILON
    diag_first = entry_xx + ridge_shift
    diag_second = entry_yy + ridge_shift
    determinant = diag_first * diag_second - entry_xy * entry_xy
    return (
        (diag_second * right_x - entry_xy * right_y) / determinant,
        (diag_first * right_y - entry_xy * right_x) / determinant,
    )


def delay_tables():
    channel_ids = np.arange(CHANNEL_COUNT)
    turns = (channel_ids[:, None] * (np.arange(NDLY)[None, :] - NDLY // 2)) % CHANNEL_COUNT
    angles = 2.0 * np.pi / CHANNEL_COUNT * turns
    cosines = np.cos(angles).reshape(N, CH, NDLY)
    sines = np.sin(angles).reshape(N, CH, NDLY)
    cos_t = cosines.transpose(0, 2, 1) / CHANNEL_COUNT
    sin_t = sines.transpose(0, 2, 1) / CHANNEL_COUNT
    ahead = np.concatenate(
        [np.concatenate([cos_t, sin_t], axis=2), np.concatenate([-sin_t, cos_t], axis=2)], axis=1
    )
    back = np.concatenate([sines, cosines], axis=2)
    return ahead.astype(np.float32), back.astype(np.float32)


def kernel(
    vis, ants, gid, sky, start, coords, ahead_hbm, back_hbm,
    gains_out, cal_out, chi_out,
    hot_spread, hot_collect, grp_spread, grp_collect, pair, gain, gain2, acc_grp, unique, unique2,
    acc_ant, rs_buf, ahead, back, ratio, part, coef, coef_buf, square_buf, tot_buf, slope_buf, chi_acc,
    vec_acc, table_sem, rs_send, rs_recv, ag_send, ag_recv, cr_send, cr_recv, ca_send, ca_recv,
    tot_send, tot_recv, slope_send, slope_recv,
):
    me = lax.axis_index("grp")
    band = lax.axis_index("chan")

    def on_grp(other):
        return (other, band)

    def on_chan(other):
        return (me, other)

    def others(body):
        def step(r, carry):
            body(r)
            return carry

        lax.fori_loop(1, N, step, 0)

    barrier = pltpu.get_barrier_semaphore()

    def greet(r):
        pl.semaphore_signal(barrier, inc=1, device_id=on_grp(lax.rem(me + r, N)), device_id_type=MESH)
        pl.semaphore_signal(barrier, inc=1, device_id=on_chan(lax.rem(band + r, N)), device_id_type=MESH)

    others(greet)

    copy_ahead = pltpu.make_async_copy(ahead_hbm.at[band], ahead, table_sem.at[0])
    copy_back = pltpu.make_async_copy(back_hbm.at[band], back, table_sem.at[1])
    copy_ahead.start()
    copy_back.start()

    vec_acc[...] = jnp.zeros_like(vec_acc)
    coords_1, coords_rest = two_parts(coords[...])
    coords_2 = coords_rest

    def build(t, carry):
        cols = pl.ds(pl.multiple_of(t * TILE, TILE), TILE)
        ant_ids = lax.broadcasted_iota(jnp.int32, (ANT_PAD, TILE), 0)
        grp_ids = lax.broadcasted_iota(jnp.int32, (GRP, TILE), 0)
        one = jnp.ones((), f32)
        nil = jnp.zeros((), f32)
        p_hot = jnp.where(ant_ids == ants[0:1, cols], one, nil).astype(bf16)
        q_hot = jnp.where(ant_ids == ants[1:2, cols], one, nil).astype(bf16)
        g_hot = jnp.where(grp_ids == gid[0:1, cols], one, nil).astype(bf16)
        for half in range(2):
            hot_spread[t, half * ANT_PAD:(half + 1) * ANT_PAD, :TILE] = p_hot
            hot_spread[t, half * ANT_PAD:(half + 1) * ANT_PAD, TILE:] = q_hot
            hot_collect[t, :, half * TILE:(half + 1) * TILE] = p_hot
            hot_collect[t, :, (2 + half) * TILE:(3 + half) * TILE] = q_hot
            grp_spread[t, half * GRP:(half + 1) * GRP, :] = g_hot
            grp_collect[t, :, half * TILE:(half + 1) * TILE] = g_hot
        diff = p_hot - q_hot
        place = dot(coords_1, diff) + dot(coords_2, diff)
        row = lax.broadcasted_iota(jnp.int32, place.shape, 0)
        place = jnp.where(row == 2, 1.0, place)
        place_1, place_2 = two_parts(place)
        vec_acc[...] += dot_last(jnp.concatenate([place_1, place_2], axis=1),
                                 jnp.concatenate([g_hot, g_hot], axis=1))
        return carry

    lax.fori_loop(0, STEPS, build, 0)

    gain[:, :, ANT_PAD - 128:] = jnp.zeros((2, CH, 128), f32)
    gain[:, :, :ANT] = start[...]

    def group_fit():
        g = gain[...].reshape(2 * CH, ANT_PAD)
        g_1, g_2 = two_parts(g)
        gain2[:, :ANT_PAD] = g_1
        gain2[:, ANT_PAD:] = g_2
        acc_grp[...] = jnp.zeros_like(acc_grp)

        def step(t, carry):
            cols = pl.ds(pl.multiple_of(t * TILE, TILE), TILE)
            pq = dot(gain2[...], hot_spread[t])
            pair[t] = pq
            a, b = pq[:CH, :TILE], pq[CH:, :TILE]
            c, d = pq[:CH, TILE:], pq[CH:, TILE:]
            x, y = vis[0, :, cols], vis[1, :, cols]
            wr = a * c + b * d
            wi = b * c - a * d
            rows = jnp.concatenate([x * wr + y * wi, y * wr - x * wi, wr * wr + wi * wi], axis=0)
            r_1, r_2 = two_parts(rows)
            acc_grp[...] += dot_last(jnp.concatenate([r_1, r_2], axis=1), grp_collect[t])
            return carry

        lax.fori_loop(0, STEPS, step, 0)
        scale = 1.0 / (acc_grp[2 * CH:, :] + RIDGE)
        u = jnp.concatenate([acc_grp[:CH, :] * scale, acc_grp[CH:2 * CH, :] * scale], axis=0)
        unique[...] = u
        u_1, u_2 = two_parts(u)
        unique2[:, :GRP] = u_1
        unique2[:, GRP:] = u_2

    def antenna_sums():
        acc_ant[...] = jnp.zeros_like(acc_ant)

        def step(t, carry):
            cols = pl.ds(pl.multiple_of(t * TILE, TILE), TILE)
            uu = dot(unique2[...], grp_spread[t])
            s, v = uu[:CH], uu[CH:]
            pq = pair[t]
            a, b = pq[:CH, :TILE], pq[CH:, :TILE]
            c, d = pq[:CH, TILE:], pq[CH:, TILE:]
            x, y = vis[0, :, cols], vis[1, :, cols]
            zr = s * x + v * y
            zi = s * y - v * x
            size = s * s + v * v
            for_p = jnp.concatenate([c * zr - d * zi, c * zi + d * zr, size * (c * c + d * d)], axis=0)
            for_q = jnp.concatenate([a * zr + b * zi, b * zr - a * zi, size * (a * a + b * b)], axis=0)
            p_1, p_2 = two_parts(for_p)
            q_1, q_2 = two_parts(for_q)
            sums = dot_last(jnp.concatenate([p_1, p_2, q_1, q_2], axis=1), hot_collect[t])
            acc_ant[...] += sums.reshape(3, CH, ANT_PAD)
            return carry

        lax.fori_loop(0, STEPS, step, 0)

    def rs_copy(block):
        rows = pl.ds(pl.multiple_of(block * ROWS, ROWS), ROWS)
        return pltpu.make_async_remote_copy(
            src_ref=acc_ant.at[:, rows, :], dst_ref=rs_buf.at[me],
            send_sem=rs_send.at[block], recv_sem=rs_recv.at[me],
            device_id=on_grp(owner_of(block)), device_id_type=MESH)

    def rs_arrival(source):
        return pltpu.make_async_remote_copy(
            src_ref=rs_buf.at[source], dst_ref=rs_buf.at[source],
            send_sem=rs_send.at[0], recv_sem=rs_recv.at[source],
            device_id=on_grp(source), device_id_type=MESH)

    def ag_copy(block, other):
        rows = pl.ds(pl.multiple_of(block * ROWS, ROWS), ROWS)
        return pltpu.make_async_remote_copy(
            src_ref=gain.at[:, rows, :], dst_ref=gain.at[:, rows, :],
            send_sem=ag_send.at[other], recv_sem=ag_recv.at[block],
            device_id=on_grp(other), device_id_type=MESH)

    def blocks(body):
        def step(k, carry):
            block = lax.rem(me + k, OWNERS)

            @pl.when(owner_of(block) != me)
            def _():
                body(block)

            return carry

        lax.fori_loop(0, OWNERS, step, 0)

    def update_gains():
        blocks(lambda block: rs_copy(block).start())

        def mine(block, carry):
            @pl.when(owner_of(block) == me)
            def _():
                rows = pl.ds(pl.multiple_of(block * ROWS, ROWS), ROWS)
                rs_buf[me] = acc_ant[:, rows, :]
                others(lambda r: rs_arrival(lax.rem(me + r, N)).wait_recv())
                total = rs_buf[0]
                for source in range(1, N):
                    total = total + rs_buf[source]
                share = 0.5 / (total[2] + RIDGE)
                gain[0, rows, :] = 0.5 * gain[0, rows, :] + total[0] * share
                gain[1, rows, :] = 0.5 * gain[1, rows, :] + total[1] * share
                others(lambda r: ag_copy(block, lax.rem(me + r, N)).start())
                others(lambda r: ag_copy(block, lax.rem(me + r, N)).wait_send())

            return carry

        lax.fori_loop(0, OWNERS, mine, 0)
        blocks(lambda block: rs_copy(block).wait_send())
        blocks(lambda block: ag_copy(block, owner_of(block)).wait_recv())

    def iteration(index, carry):
        group_fit()
        antenna_sums()

        @pl.when(index == 0)
        def _():
            pl.semaphore_wait(barrier, 2 * (N - 1))

        update_gains()
        return carry

    lax.fori_loop(0, ITERS, iteration, 0)
    group_fit()
    gains_out[...] = gain[:, :, :ANT]

    ur, ui = unique[:CH, :], unique[CH:, :]
    sr, si = sky[0], sky[1]
    ratio[:CH, :] = ur * sr + ui * si
    ratio[CH:, :] = ui * sr - ur * si
    copy_ahead.wait()
    part[...] = jnp.dot(ahead[...], ratio[...], precision=HIGHEST, preferred_element_type=f32)

    def cr_copy(other):
        rows = pl.ds(pl.multiple_of(other * 8, 8), 8)
        return pltpu.make_async_remote_copy(
            src_ref=part.at[rows, :], dst_ref=coef_buf.at[band],
            send_sem=cr_send.at[other], recv_sem=cr_recv.at[band],
            device_id=on_chan(other), device_id_type=MESH)

    def cr_arrival(source):
        return pltpu.make_async_remote_copy(
            src_ref=coef_buf.at[source], dst_ref=coef_buf.at[source],
            send_sem=cr_send.at[0], recv_sem=cr_recv.at[source],
            device_id=on_chan(source), device_id_type=MESH)

    def ca_copy(source, other):
        rows = pl.ds(pl.multiple_of(source * 8, 8), 8)
        return pltpu.make_async_remote_copy(
            src_ref=coef.at[rows, :], dst_ref=coef.at[rows, :],
            send_sem=ca_send.at[other], recv_sem=ca_recv.at[source],
            device_id=on_chan(other), device_id_type=MESH)

    others(lambda r: cr_copy(lax.rem(band + r, N)).start())
    my_rows = pl.ds(pl.multiple_of(band * 8, 8), 8)
    coef_buf[band] = part[my_rows, :]
    others(lambda r: cr_arrival(lax.rem(band + r, N)).wait_recv())
    others(lambda r: cr_copy(lax.rem(band + r, N)).wait_send())
    total_coef = coef_buf[0]
    for source in range(1, N):
        total_coef = total_coef + coef_buf[source]
    coef[my_rows, :] = total_coef
    others(lambda r: ca_copy(band, lax.rem(band + r, N)).start())

    chi_acc[...] = jnp.zeros_like(chi_acc)

    def misfit(t, carry):
        cols = pl.ds(pl.multiple_of(t * TILE, TILE), TILE)
        uu = dot(unique2[...], grp_spread[t])
        s, v = uu[:CH], uu[CH:]
        pq = pair[t]
        a, b = pq[:CH, :TILE], pq[CH:, :TILE]
        c, d = pq[:CH, TILE:], pq[CH:, TILE:]
        wr = a * c + b * d
        wi = b * c - a * d
        er = vis[0, :, cols] - (wr * s - wi * v)
        ei = vis[1, :, cols] - (wr * v + wi * s)
        e = er * er + ei * ei
        chi_acc[...] += e[:, :128] + e[:, 128:]
        return carry

    lax.fori_loop(0, STEPS, misfit, 0)

    east = vec_acc[0:1, :] / vec_acc[2:3, :]
    north = vec_acc[1:2, :] / vec_acc[2:3, :]
    model = sr * sr + si * si
    squared = model * model
    copy_back.wait()
    others(lambda r: ca_copy(lax.rem(band + r, N), band).wait_recv())
    others(lambda r: ca_copy(band, lax.rem(band + r, N)).wait_send())
    phases = jnp.dot(back[...], coef[...], precision=HIGHEST, preferred_element_type=f32)

    weighted = model * phases
    fields = [
        ur * ur + ui * ui, model, squared * (east * east), squared * (east * north),
        squared * (north * north), weighted * east, weighted * north, chi_acc[...],
    ]
    lane = lax.broadcasted_iota(jnp.int32, (CH, 128), 1)
    table = jnp.zeros((CH, 128), f32)
    for place, field in enumerate(fields):
        table = jnp.where(lane == place, jnp.sum(field, axis=1, keepdims=True), table)
    square_buf[CH:, :] = jnp.zeros((128 - CH, 128), f32)
    square_buf[:CH, :] = table
    tot_buf[me] = square_buf[...].T[:8, :]

    def tot_copy(source, other):
        return pltpu.make_async_remote_copy(
            src_ref=tot_buf.at[source], dst_ref=tot_buf.at[source],
            send_sem=tot_send.at[other], recv_sem=tot_recv.at[source],
            device_id=on_grp(other), device_id_type=MESH)

    others(lambda r: tot_copy(me, lax.rem(me + r, N)).start())
    others(lambda r: tot_copy(lax.rem(me + r, N), me).wait_recv())
    others(lambda r: tot_copy(me, lax.rem(me + r, N)).wait_send())
    totals = tot_buf[0]
    for source in range(1, N):
        totals = totals + tot_buf[source]
    chi_out[...] = totals[7:8, :CH]

    channel = band * CH + lax.broadcasted_iota(jnp.int32, (1, 128), 1)
    frequency = 1.0 + channel.astype(f32) * (1.0 / CHANNEL_COUNT)
    squares = frequency * frequency
    slope_buf[band] = jnp.concatenate(
        [squares * totals[2:3], squares * totals[3:4], squares * totals[4:5],
         frequency * totals[5:6], frequency * totals[6:7], jnp.zeros((3, 128), f32)], axis=0)

    def slope_copy(source, other):
        return pltpu.make_async_remote_copy(
            src_ref=slope_buf.at[source], dst_ref=slope_buf.at[source],
            send_sem=slope_send.at[other], recv_sem=slope_recv.at[source],
            device_id=on_chan(other), device_id_type=MESH)

    others(lambda r: slope_copy(band, lax.rem(band + r, N)).start())
    tilt_east, tilt_north = solve_pair(
        totals[2:3], totals[3:4], totals[4:5], totals[5:6], totals[6:7])
    amplitude = jnp.sqrt((totals[0:1] + EPSILON) / (totals[1:2] + EPSILON))
    scale = 1.0 / amplitude
    others(lambda r: slope_copy(lax.rem(band + r, N), band).wait_recv())
    others(lambda r: slope_copy(band, lax.rem(band + r, N)).wait_send())
    slopes = slope_buf[0]
    for source in range(1, N):
        slopes = slopes + slope_buf[source]
    terms = jnp.sum(slopes, axis=1, keepdims=True)
    slope_east, slope_north = solve_pair(
        terms[0:1], terms[1:2], terms[2:3], terms[3:4], terms[4:5])
    tilt_east = tilt_east - frequency * slope_east
    tilt_north = tilt_north - frequency * slope_north
    square_buf[0:8, :] = jnp.concatenate(
        [frequency, tilt_east, tilt_north, scale, jnp.zeros((4, 128), f32)], axis=0)
    columns = square_buf[...].T[:CH, :]
    along = slope_east * east + slope_north * north
    turn = columns[:, 0:1] * along + columns[:, 1:2] * east + columns[:, 2:3] * north
    rotation_cos = jnp.cos(turn) * columns[:, 3:4]
    rotation_sin = jnp.sin(turn) * columns[:, 3:4]
    cal_out[0] = ur * rotation_cos + ui * rotation_sin
    cal_out[1] = ui * rotation_cos - ur * rotation_sin


def per_device(ahead, back, vis, ants, gid, sky, start, coords):
    coords = jnp.pad(coords, ((0, 6), (0, ANT_PAD - ANT)))
    vmem = pl.BlockSpec(memory_space=pltpu.VMEM)
    dma = pltpu.SemaphoreType.DMA
    gains, cal, chi = pl.pallas_call(
        kernel,
        out_shape=(
            jax.ShapeDtypeStruct((2, CH, ANT), f32),
            jax.ShapeDtypeStruct((2, CH, GRP), f32),
            jax.ShapeDtypeStruct((1, CH), f32),
        ),
        in_specs=[vmem] * 6 + [pl.BlockSpec(memory_space=pl.ANY)] * 2,
        out_specs=(vmem, vmem, vmem),
        scratch_shapes=[
            pltpu.VMEM((STEPS, 2 * ANT_PAD, 2 * TILE), bf16),
            pltpu.VMEM((STEPS, ANT_PAD, 4 * TILE), bf16),
            pltpu.VMEM((STEPS, 2 * GRP, TILE), bf16),
            pltpu.VMEM((STEPS, GRP, 2 * TILE), bf16),
            pltpu.VMEM((STEPS, 2 * CH, 2 * TILE), f32),
            pltpu.VMEM((2, CH, ANT_PAD), f32),
            pltpu.VMEM((2 * CH, 2 * ANT_PAD), bf16),
            pltpu.VMEM((3 * CH, GRP), f32),
            pltpu.VMEM((2 * CH, GRP), f32),
            pltpu.VMEM((2 * CH, 2 * GRP), bf16),
            pltpu.VMEM((3, CH, ANT_PAD), f32),
            pltpu.VMEM((N, 3, ROWS, ANT_PAD), f32),
            pltpu.VMEM((2 * NDLY, 2 * CH), f32),
            pltpu.VMEM((CH, 2 * NDLY), f32),
            pltpu.VMEM((2 * CH, GRP), f32),
            pltpu.VMEM((2 * NDLY, GRP), f32),
            pltpu.VMEM((2 * NDLY, GRP), f32),
            pltpu.VMEM((N, 8, GRP), f32),
            pltpu.VMEM((128, 128), f32),
            pltpu.VMEM((N, 8, 128), f32),
            pltpu.VMEM((N, 8, 128), f32),
            pltpu.VMEM((CH, 128), f32),
            pltpu.VMEM((8, GRP), f32),
            dma((2,)),
        ] + [dma((N,))] * 12,
        compiler_params=pltpu.CompilerParams(
            collective_id=0, has_side_effects=True, vmem_limit_bytes=48 * 1024 * 1024),
        cost_estimate=pl.CostEstimate(flops=20_000_000_000, bytes_accessed=4_000_000, transcendentals=0),
    )(vis, ants, gid, sky, start, coords, ahead, back)
    return gains, cal, chi.reshape(CH)


def solution(mesh):
    ahead, back = delay_tables()

    def program(vis, ants, gid, sky, start, coords):
        return jax.shard_map(
            functools.partial(per_device, ahead, back),
            mesh=mesh,
            in_specs=(
                P(None, "chan", "grp"),
                P(None, "grp"),
                P("grp", None),
                P(None, "chan", "grp"),
                P(None, "chan", None),
                P(),
            ),
            out_specs=(P(None, "chan", None), P(None, "chan", "grp"), P("chan")),
            check_vma=False,
        )(vis, ants, gid, sky, start, coords)

    return program
```

```python
import functools

import jax
import jax.numpy as jnp
import numpy as np
from jax import lax
from jax.experimental import pallas as pl
from jax.experimental.pallas import tpu as pltpu
from jax.sharding import PartitionSpec as P

CHANNEL_COUNT = 1536
NDLY = 64
ITERS = 4
RIDGE = 0.5
EPSILON = 1e-06

N = 16
ANT = 350
ANT_PAD = 384
CH = 96
CHUNKS = 3
CHK = CH // CHUNKS
BL = 2048
GRP = 128
TILE = 256
STEPS = BL // TILE
OWN = GRP // N
LANES = 128
UNITS = (CHK // 8) * (ANT_PAD // LANES)

MESH = pl.DeviceIdType.MESH
HIGHEST = lax.Precision.HIGHEST
f32 = jnp.float32
bf16 = jnp.bfloat16


def owner_of(unit):
    return unit + 1 + unit // 4


def two_parts(number):
    first = number.astype(bf16)
    rest = (number - first.astype(f32)).astype(bf16)
    return jnp.concatenate([first, rest], axis=0)


def joined(parts):
    half = parts.shape[0] // 2
    return parts[:half] + parts[half:]


def dot(left, right):
    return jnp.dot(left, right, preferred_element_type=f32)


def dot_last(left, right):
    return lax.dot_general(left, right, (((1,), (1,)), ((), ())), preferred_element_type=f32)


def exact_dot(left, right):
    return jnp.dot(left, right, precision=HIGHEST, preferred_element_type=f32)


def solve_pair(entry_xx, entry_xy, entry_yy, right_x, right_y):
    ridge_shift = 0.001 * (entry_xx + entry_yy) + EPSILON
    diag_first = entry_xx + ridge_shift
    diag_second = entry_yy + ridge_shift
    determinant = diag_first * diag_second - entry_xy * entry_xy
    return (
        (diag_second * right_x - entry_xy * right_y) / determinant,
        (diag_first * right_y - entry_xy * right_x) / determinant,
    )


def delay_tables():
    channel_ids = np.arange(CHANNEL_COUNT)
    turns = (channel_ids[:, None] * (np.arange(NDLY)[None, :] - NDLY // 2)) % CHANNEL_COUNT
    angles = 2.0 * np.pi / CHANNEL_COUNT * turns
    cosines = np.cos(angles).reshape(N, CH, NDLY).transpose(0, 2, 1)
    sines = np.sin(angles).reshape(N, CH, NDLY).transpose(0, 2, 1)
    ahead = np.concatenate(
        [np.concatenate([cosines, sines], axis=2), np.concatenate([-sines, cosines], axis=2)], axis=1
    )
    back = np.zeros((2 * NDLY, N, LANES))
    back[:NDLY, :, :CH] = sines.transpose(1, 0, 2)
    back[NDLY:, :, :CH] = cosines.transpose(1, 0, 2)
    return (ahead / CHANNEL_COUNT).astype(np.float32), back.reshape(2 * NDLY, N * LANES).astype(np.float32)


def kernel(
    vis_hbm, ants_hbm, gid_hbm, sky_hbm, start_hbm, coords_hbm, ahead_hbm, back_hbm,
    gains_out, cal_out, chi_out,
    vis, ants, gid, sky, start, coords, ahead, back,
    hot, grp_hot, pair, gain, gain2, acc_grp, unique, unique2, acc_sum, acc_ant, rs_buf,
    ratio, part, coef_buf, model_t, model_band, square, vec_acc, vec_t, chi_acc,
    band_send_buf, band_buf, tot_buf,
    load_sem, rs_send, rs_recv, ag_send, ag_recv, mod_send, mod_recv, cr_send, cr_recv,
    band_send, band_recv, tot_send, tot_recv,
):
    me = lax.axis_index("grp")
    band = lax.axis_index("chan")
    i_own = lax.rem(me, 5) != 0
    my_unit = me - 1 - me // 5

    def others(body):
        for r in range(1, N):
            body(r)

    def grp_other(r):
        return lax.rem(me + r, N)

    def chan_other(r):
        return lax.rem(band + r, N)

    loads = [
        pltpu.make_async_copy(ants_hbm, ants, load_sem.at[0]),
        pltpu.make_async_copy(gid_hbm, gid, load_sem.at[1]),
        pltpu.make_async_copy(coords_hbm, coords, load_sem.at[2]),
        pltpu.make_async_copy(start_hbm, start, load_sem.at[3]),
        pltpu.make_async_copy(vis_hbm, vis, load_sem.at[4]),
        pltpu.make_async_copy(sky_hbm, sky, load_sem.at[5]),
        pltpu.make_async_copy(ahead_hbm.at[band], ahead, load_sem.at[6]),
        pltpu.make_async_copy(back_hbm, back, load_sem.at[7]),
    ]
    for load in loads:
        load.start()

    barrier = pltpu.get_barrier_semaphore()

    def greet(r):
        pl.semaphore_signal(barrier, inc=1, device_id=(grp_other(r), band), device_id_type=MESH)
        pl.semaphore_signal(barrier, inc=1, device_id=(me, chan_other(r)), device_id_type=MESH)

    others(greet)

    loads[0].wait()
    loads[1].wait()
    loads[2].wait()
    vec_acc[...] = jnp.zeros_like(vec_acc)
    gain[:, :, ANT_PAD - LANES:] = jnp.zeros((2, CH, LANES), f32)
    gain[0, :8, :] = jnp.zeros((8, ANT_PAD), f32)
    gain[0, 0:2, :ANT] = coords[...]
    places = two_parts(gain[0, :8, :])

    def build(t, carry):
        cols = pl.ds(pl.multiple_of(t * TILE, TILE), TILE)
        ant_ids = lax.broadcasted_iota(jnp.int32, (ANT_PAD, TILE), 0)
        grp_ids = lax.broadcasted_iota(jnp.int32, (GRP, TILE), 0)
        p_hot = jnp.where(ant_ids == ants[0:1, cols], 1.0, 0.0).astype(bf16)
        q_hot = jnp.where(ant_ids == ants[1:2, cols], 1.0, 0.0).astype(bf16)
        g_hot = jnp.where(grp_ids == gid[0:1, cols], 1.0, 0.0).astype(bf16)
        hot[t, :, :TILE] = p_hot
        hot[t, :, TILE:] = q_hot
        grp_hot[t] = g_hot
        place = joined(dot(places, p_hot - q_hot))
        row = lax.broadcasted_iota(jnp.int32, place.shape, 0)
        place = jnp.where(row == 2, 1.0, place)
        vec_acc[...] += joined(dot_last(two_parts(place), g_hot))
        return carry

    lax.fori_loop(0, STEPS, build, 0)

    loads[3].wait()
    gain[:, :, :ANT] = start[...]
    loads[4].wait()

    def rows_of(chunk):
        return pl.ds(pl.multiple_of(chunk * CHK, CHK), CHK)

    def group_fit(chunk):
        mine = rows_of(chunk)
        gain2[...] = two_parts(gain[:, mine, :].reshape(2 * CHK, ANT_PAD))
        acc_grp[...] = jnp.zeros_like(acc_grp)

        def step(t, carry):
            cols = pl.ds(pl.multiple_of(t * TILE, TILE), TILE)
            pq = joined(dot(gain2[...], hot[t]))
            pair[t] = pq
            a, b = pq[:CHK, :TILE], pq[CHK:, :TILE]
            c, d = pq[:CHK, TILE:], pq[CHK:, TILE:]
            x, y = vis[0, mine, cols], vis[1, mine, cols]
            wr = a * c + b * d
            wi = b * c - a * d
            rows = jnp.concatenate([x * wr + y * wi, y * wr - x * wi, wr * wr + wi * wi], axis=0)
            acc_grp[...] += dot_last(two_parts(rows), grp_hot[t])
            return carry

        lax.fori_loop(0, STEPS, step, 0, unroll=8)
        sums = joined(acc_grp[...])
        scale = 1.0 / (sums[2 * CHK:] + RIDGE)
        ur, ui = sums[:CHK] * scale, sums[CHK:2 * CHK] * scale
        unique[0, mine, :] = ur
        unique[1, mine, :] = ui
        unique2[...] = two_parts(jnp.concatenate([ur, ui], axis=0))

    def antenna_sums(chunk):
        mine = rows_of(chunk)
        acc_sum[...] = jnp.zeros_like(acc_sum)

        def step(t, carry):
            cols = pl.ds(pl.multiple_of(t * TILE, TILE), TILE)
            uu = joined(dot(unique2[...], grp_hot[t]))
            s, v = uu[:CHK], uu[CHK:]
            pq = pair[t]
            a, b = pq[:CHK, :TILE], pq[CHK:, :TILE]
            c, d = pq[:CHK, TILE:], pq[CHK:, TILE:]
            x, y = vis[0, mine, cols], vis[1, mine, cols]
            zr = s * x + v * y
            zi = s * y - v * x
            size = s * s + v * v
            for_p = jnp.concatenate([c * zr - d * zi, c * zi + d * zr, size * (c * c + d * d)], axis=0)
            for_q = jnp.concatenate([a * zr + b * zi, b * zr - a * zi, size * (a * a + b * b)], axis=0)
            acc_sum[...] += dot_last(two_parts(jnp.concatenate([for_p, for_q], axis=1)), hot[t])
            return carry

        lax.fori_loop(0, STEPS, step, 0, unroll=8)
        acc_ant[chunk] = joined(acc_sum[...]).reshape(3, CHK, ANT_PAD)

    def misfit(chunk):
        mine = rows_of(chunk)
        chi_acc[mine, :] = jnp.zeros((CHK, LANES), f32)

        def step(t, carry):
            cols = pl.ds(pl.multiple_of(t * TILE, TILE), TILE)
            uu = joined(dot(unique2[...], grp_hot[t]))
            s, v = uu[:CHK], uu[CHK:]
            pq = pair[t]
            a, b = pq[:CHK, :TILE], pq[CHK:, :TILE]
            c, d = pq[:CHK, TILE:], pq[CHK:, TILE:]
            wr = a * c + b * d
            wi = b * c - a * d
            er = vis[0, mine, cols] - (wr * s - wi * v)
            ei = vis[1, mine, cols] - (wr * v + wi * s)
            e = er * er + ei * ei
            chi_acc[mine, :] += e[:, :LANES] + e[:, LANES:]
            return carry

        lax.fori_loop(0, STEPS, step, 0, unroll=8)

    def place_of(unit):
        across = ANT_PAD // LANES
        tile = unit // across
        lanes = pl.ds(pl.multiple_of((unit - tile * across) * LANES, LANES), LANES)
        return tile * 8, lanes

    def rs_copy(chunk, unit):
        row, lanes = place_of(unit)
        return pltpu.make_async_remote_copy(
            src_ref=acc_ant.at[chunk, :, pl.ds(pl.multiple_of(row, 8), 8), lanes],
            dst_ref=rs_buf.at[chunk, me],
            send_sem=rs_send.at[chunk, unit], recv_sem=rs_recv.at[chunk, me],
            device_id=(owner_of(unit), band), device_id_type=MESH)

    def rs_arrival(chunk, source):
        return pltpu.make_async_remote_copy(
            src_ref=rs_buf.at[chunk, source], dst_ref=rs_buf.at[chunk, source],
            send_sem=rs_send.at[chunk, 0], recv_sem=rs_recv.at[chunk, source],
            device_id=(source, band), device_id_type=MESH)

    def ag_copy(chunk, unit, other):
        row, lanes = place_of(unit)
        block = gain.at[:, pl.ds(pl.multiple_of(chunk * CHK + row, 8), 8), lanes]
        return pltpu.make_async_remote_copy(
            src_ref=block, dst_ref=block,
            send_sem=ag_send.at[chunk, other], recv_sem=ag_recv.at[chunk, unit],
            device_id=(other, band), device_id_type=MESH)

    def units(body):
        def step(k, carry):
            unit = lax.rem(me + k, UNITS)

            @pl.when(owner_of(unit) != me)
            def _():
                body(unit)

            return carry

        lax.fori_loop(0, UNITS, step, 0)

    def send_sums(chunk):
        units(lambda unit: rs_copy(chunk, unit).start())

    def update_gains(chunk):
        @pl.when(i_own)
        def _():
            row, lanes = place_of(my_unit)
            rs_buf[chunk, me] = acc_ant[chunk, :, pl.ds(pl.multiple_of(row, 8), 8), lanes]
            others(lambda r: rs_arrival(chunk, grp_other(r)).wait_recv())
            total = rs_buf[chunk, 0]
            for source in range(1, N):
                total = total + rs_buf[chunk, source]
            share = 0.5 / (total[2] + RIDGE)
            here = pl.ds(pl.multiple_of(chunk * CHK + row, 8), 8)
            gain[0, here, lanes] = 0.5 * gain[0, here, lanes] + total[0] * share
            gain[1, here, lanes] = 0.5 * gain[1, here, lanes] + total[1] * share
            others(lambda r: ag_copy(chunk, my_unit, grp_other(r)).start())

    def await_gains(chunk):
        units(lambda unit: ag_copy(chunk, unit, owner_of(unit)).wait_recv())
        units(lambda unit: rs_copy(chunk, unit).wait_send())

        @pl.when(i_own)
        def _():
            others(lambda r: ag_copy(chunk, my_unit, grp_other(r)).wait_send())

    def mod_copy(source, other):
        return pltpu.make_async_remote_copy(
            src_ref=model_t.at[pl.ds(pl.multiple_of(other * OWN, OWN), OWN), :],
            dst_ref=model_band.at[:, pl.ds(pl.multiple_of(source * LANES, LANES), LANES)],
            send_sem=mod_send.at[other], recv_sem=mod_recv.at[source],
            device_id=(me, other), device_id_type=MESH)

    def iteration(s, carry):
        chunk = lax.rem(s, CHUNKS)

        @pl.when(s >= CHUNKS)
        def _():
            await_gains(chunk)

        group_fit(chunk)
        antenna_sums(chunk)

        @pl.when(s == 0)
        def _():
            pl.semaphore_wait(barrier, 2 * (N - 1))

        send_sums(chunk)

        @pl.when(s >= 1)
        def _():
            update_gains(lax.rem(s + CHUNKS - 1, CHUNKS))

        @pl.when(s == 0)
        def _():
            loads[5].wait()
            model = sky[0] * sky[0] + sky[1] * sky[1]
            square[CH:, :] = jnp.zeros((LANES - CH, LANES), f32)
            square[:CH, :] = model
            model_t[...] = square[...].T
            own_rows = pl.ds(pl.multiple_of(band * OWN, OWN), OWN)
            own_lanes = pl.ds(pl.multiple_of(band * LANES, LANES), LANES)
            model_band[:, own_lanes] = model_t[own_rows, :]
            others(lambda r: mod_copy(band, chan_other(r)).start())

        return carry

    lax.fori_loop(0, ITERS * CHUNKS, iteration, 0)

    def last(chunk, carry):
        await_gains(chunk)
        group_fit(chunk)

        @pl.when(chunk == 0)
        def _():
            update_gains(CHUNKS - 1)

        misfit(chunk)
        return carry

    lax.fori_loop(0, CHUNKS, last, 0)

    ur, ui = unique[0], unique[1]
    sr, si = sky[0], sky[1]
    ratio[:CH, :] = ur * sr + ui * si
    ratio[CH:, :] = ui * sr - ur * si
    loads[6].wait()
    part[...] = exact_dot(ahead[...], ratio[...]).T

    def cr_copy(source, other):
        return pltpu.make_async_remote_copy(
            src_ref=part.at[pl.ds(pl.multiple_of(other * OWN, OWN), OWN), :], dst_ref=coef_buf.at[source],
            send_sem=cr_send.at[other], recv_sem=cr_recv.at[source],
            device_id=(me, other), device_id_type=MESH)

    others(lambda r: cr_copy(band, chan_other(r)).start())
    coef_buf[band] = part[pl.ds(pl.multiple_of(band * OWN, OWN), OWN), :]

    gains_out[...] = gain[:, :, :ANT]
    east = vec_acc[0:1, :] / vec_acc[2:3, :]
    north = vec_acc[1:2, :] / vec_acc[2:3, :]
    square[...] = jnp.zeros_like(square)
    square[0:1, :] = east
    square[1:2, :] = north
    vec_t[...] = square[...].T
    model = sr * sr + si * si
    squared = model * model
    fields = [
        ur * ur + ui * ui, model, squared * (east * east), squared * (east * north),
        squared * (north * north), chi_acc[...],
    ]
    lane = lax.broadcasted_iota(jnp.int32, (CH, LANES), 1)
    table = jnp.zeros((CH, LANES), f32)
    for place, field in enumerate(fields):
        table = jnp.where(lane == place, jnp.sum(field, axis=1, keepdims=True), table)
    square[CH:, :] = jnp.zeros((LANES - CH, LANES), f32)
    square[:CH, :] = table
    local = square[...].T[:8, :]

    channel = band * CH + lax.broadcasted_iota(jnp.int32, (1, LANES), 1)
    frequency = 1.0 + channel.astype(f32) * (1.0 / CHANNEL_COUNT)
    squares = frequency * frequency
    slope_parts = squares * local[2:5]
    at = lax.broadcasted_iota(jnp.int32, (1, N * LANES), 1)
    band_channel = (at // LANES) * CH + lax.rem(at, LANES)
    band_frequency = 1.0 + band_channel.astype(f32) * (1.0 / CHANNEL_COUNT)
    my_groups = vec_t[pl.ds(pl.multiple_of(band * OWN, OWN), OWN), :]

    loads[7].wait()
    others(lambda r: mod_copy(chan_other(r), band).wait_recv())
    others(lambda r: mod_copy(band, chan_other(r)).wait_send())
    weights_east = model_band[...] * my_groups[:, 0:1]
    weights_north = model_band[...] * my_groups[:, 1:2]

    others(lambda r: cr_copy(chan_other(r), band).wait_recv())
    coef = coef_buf[0]
    for source in range(1, N):
        coef = coef + coef_buf[source]
    phases = exact_dot(coef, back[...])
    right_east = jnp.sum(weights_east * phases, axis=0, keepdims=True)
    right_north = jnp.sum(weights_north * phases, axis=0, keepdims=True)
    slope_east = jnp.sum(band_frequency * right_east, axis=1, keepdims=True)
    slope_north = jnp.sum(band_frequency * right_north, axis=1, keepdims=True)
    first_lane = lax.broadcasted_iota(jnp.int32, (1, LANES), 1) == 0
    slope_rows = jnp.concatenate(
        [jnp.where(first_lane, slope_east, 0.0), jnp.where(first_lane, slope_north, 0.0),
         slope_parts, jnp.zeros((1, LANES), f32)], axis=0)
    for other in range(N):
        lanes = slice(other * LANES, (other + 1) * LANES)
        band_send_buf[other] = jnp.concatenate([right_east[:, lanes], right_north[:, lanes], slope_rows], axis=0)

    def band_copy(source, other):
        return pltpu.make_async_remote_copy(
            src_ref=band_send_buf.at[other], dst_ref=band_buf.at[source],
            send_sem=band_send.at[other], recv_sem=band_recv.at[source],
            device_id=(me, other), device_id_type=MESH)

    others(lambda r: band_copy(band, chan_other(r)).start())
    band_buf[band] = band_send_buf[band]
    others(lambda r: cr_copy(band, chan_other(r)).wait_send())
    others(lambda r: band_copy(chan_other(r), band).wait_recv())
    sums = band_buf[0]
    for source in range(1, N):
        sums = sums + band_buf[source]

    tot_buf[me] = jnp.concatenate(
        [local[0:5], sums[0:2], local[5:6], sums[2:7], jnp.zeros((3, LANES), f32)], axis=0)

    def tot_copy(source, other):
        return pltpu.make_async_remote_copy(
            src_ref=tot_buf.at[source], dst_ref=tot_buf.at[source],
            send_sem=tot_send.at[other], recv_sem=tot_recv.at[source],
            device_id=(other, band), device_id_type=MESH)

    others(lambda r: tot_copy(me, grp_other(r)).start())
    others(lambda r: band_copy(band, chan_other(r)).wait_send())
    others(lambda r: tot_copy(grp_other(r), me).wait_recv())
    totals = tot_buf[0]
    for source in range(1, N):
        totals = totals + tot_buf[source]
    others(lambda r: tot_copy(me, grp_other(r)).wait_send())
    chi_out[...] = totals[7:8, :CH]

    terms = jnp.sum(totals[8:16], axis=1, keepdims=True)
    slope_east, slope_north = solve_pair(
        terms[2:3], terms[3:4], terms[4:5], terms[0:1], terms[1:2])
    tilt_east, tilt_north = solve_pair(
        totals[2:3], totals[3:4], totals[4:5], totals[5:6], totals[6:7])
    tilt_east = tilt_east - frequency * slope_east
    tilt_north = tilt_north - frequency * slope_north
    amplitude = jnp.sqrt((totals[0:1] + EPSILON) / (totals[1:2] + EPSILON))
    square[0:8, :] = jnp.concatenate(
        [frequency, tilt_east, tilt_north, 1.0 / amplitude, jnp.zeros((4, LANES), f32)], axis=0)
    columns = square[...].T[:CH, :]
    along = slope_east * east + slope_north * north
    turn = columns[:, 0:1] * along + columns[:, 1:2] * east + columns[:, 2:3] * north
    rotation_cos = jnp.cos(turn) * columns[:, 3:4]
    rotation_sin = jnp.sin(turn) * columns[:, 3:4]
    cal_out[0] = ur * rotation_cos + ui * rotation_sin
    cal_out[1] = ui * rotation_cos - ur * rotation_sin


def per_device(ahead, back, vis, ants, gid, sky, start, coords):
    vmem = pl.BlockSpec(memory_space=pltpu.VMEM)
    hbm = pl.BlockSpec(memory_space=pltpu.HBM)
    dma = pltpu.SemaphoreType.DMA
    gains, cal, chi = pl.pallas_call(
        kernel,
        out_shape=(
            jax.ShapeDtypeStruct((2, CH, ANT), f32),
            jax.ShapeDtypeStruct((2, CH, GRP), f32),
            jax.ShapeDtypeStruct((1, CH), f32),
        ),
        in_specs=[hbm] * 8,
        out_specs=(vmem, vmem, vmem),
        scratch_shapes=[
            pltpu.VMEM((2, CH, BL), f32),
            pltpu.VMEM((2, BL), jnp.int32),
            pltpu.VMEM((1, BL), jnp.int32),
            pltpu.VMEM((2, CH, GRP), f32),
            pltpu.VMEM((2, CH, ANT), f32),
            pltpu.VMEM((2, ANT), f32),
            pltpu.VMEM((2 * NDLY, 2 * CH), f32),
            pltpu.VMEM((2 * NDLY, N * LANES), f32),
            pltpu.VMEM((STEPS, ANT_PAD, 2 * TILE), bf16),
            pltpu.VMEM((STEPS, GRP, TILE), bf16),
            pltpu.VMEM((STEPS, 2 * CHK, 2 * TILE), f32),
            pltpu.VMEM((2, CH, ANT_PAD), f32),
            pltpu.VMEM((4 * CHK, ANT_PAD), bf16),
            pltpu.VMEM((6 * CHK, GRP), f32),
            pltpu.VMEM((2, CH, GRP), f32),
            pltpu.VMEM((4 * CHK, GRP), bf16),
            pltpu.VMEM((6 * CHK, ANT_PAD), f32),
            pltpu.VMEM((CHUNKS, 3, CHK, ANT_PAD), f32),
            pltpu.VMEM((CHUNKS, N, 3, 8, LANES), f32),
            pltpu.VMEM((2 * CH, GRP), f32),
            pltpu.VMEM((GRP, 2 * NDLY), f32),
            pltpu.VMEM((N, OWN, 2 * NDLY), f32),
            pltpu.VMEM((GRP, LANES), f32),
            pltpu.VMEM((OWN, N * LANES), f32),
            pltpu.VMEM((LANES, LANES), f32),
            pltpu.VMEM((8, GRP), f32),
            pltpu.VMEM((GRP, LANES), f32),
            pltpu.VMEM((CH, LANES), f32),
            pltpu.VMEM((N, 8, LANES), f32),
            pltpu.VMEM((N, 8, LANES), f32),
            pltpu.VMEM((N, 16, LANES), f32),
            dma((8,)),
            dma((CHUNKS, UNITS)), dma((CHUNKS, N)), dma((CHUNKS, N)), dma((CHUNKS, UNITS)),
        ] + [dma((N,))] * 8,
        compiler_params=pltpu.CompilerParams(
            collective_id=0, has_side_effects=True, vmem_limit_bytes=48 * 1024 * 1024),
        cost_estimate=pl.CostEstimate(flops=20_000_000_000, bytes_accessed=4_000_000, transcendentals=0),
    )(vis, ants, gid, sky, start, coords, ahead, back)
    return gains, cal, chi.reshape(CH)


def solution(mesh):
    ahead, back = delay_tables()

    def program(vis, ants, gid, sky, start, coords):
        return jax.shard_map(
            functools.partial(per_device, ahead, back),
            mesh=mesh,
            in_specs=(
                P(None, "chan", "grp"),
                P(None, "grp"),
                P("grp", None),
                P(None, "chan", "grp"),
                P(None, "chan", None),
                P(),
            ),
            out_specs=(P(None, "chan", None), P(None, "chan", "grp"), P("chan")),
            check_vma=False,
        )(vis, ants, gid, sky, start, coords)

    return program
```

```python
import functools

import jax
import jax.numpy as jnp
import numpy as np
from jax import lax
from jax.experimental import pallas as pl
from jax.experimental.pallas import tpu as pltpu
from jax.sharding import PartitionSpec as P

CHANNEL_COUNT = 1536
NDLY = 64
ITERS = 4
RIDGE = 0.5
EPSILON = 1e-06

N = 16
ANT = 350
ANT_PAD = 384
CH = 96
CHUNKS = 3
CHK = CH // CHUNKS
BL = 2048
GRP = 128
TILE = 256
STEPS = BL // TILE
SPAN = 8
OWN = GRP // N
LANES = 128
UNITS = (CHK // 8) * (ANT_PAD // LANES)

GRP_STEPS = sorted(
    ((dx, dy) for dx in range(4) for dy in range(4) if dx or dy),
    key=lambda step: -min(step[0], 4 - step[0]) - min(step[1], 4 - step[1]))
CHAN_STEPS = sorted(
    ((dz, core) for dz in range(8) for core in range(2) if dz or core),
    key=lambda step: -2 * min(step[0], 8 - step[0]) - step[1])

MESH = pl.DeviceIdType.MESH
HIGHEST = lax.Precision.HIGHEST
f32 = jnp.float32
bf16 = jnp.bfloat16


def owner_of(unit):
    return unit + 1 + unit // 4


def two_parts(number):
    first = number.astype(bf16)
    rest = (number - first.astype(f32)).astype(bf16)
    return jnp.concatenate([first, rest], axis=0)


def joined(parts):
    half = parts.shape[0] // 2
    return parts[:half] + parts[half:]


def dot(left, right):
    return jnp.dot(left, right, preferred_element_type=f32)


def dot_last(left, right):
    return lax.dot_general(left, right, (((1,), (1,)), ((), ())), preferred_element_type=f32)


def exact_dot(left, right):
    return jnp.dot(left, right, precision=HIGHEST, preferred_element_type=f32)


def solve_pair(entry_xx, entry_xy, entry_yy, right_x, right_y):
    ridge_shift = 0.001 * (entry_xx + entry_yy) + EPSILON
    diag_first = entry_xx + ridge_shift
    diag_second = entry_yy + ridge_shift
    determinant = diag_first * diag_second - entry_xy * entry_xy
    return (
        (diag_second * right_x - entry_xy * right_y) / determinant,
        (diag_first * right_y - entry_xy * right_x) / determinant,
    )


def delay_tables():
    channel_ids = np.arange(CHANNEL_COUNT)
    turns = (channel_ids[:, None] * (np.arange(NDLY)[None, :] - NDLY // 2)) % CHANNEL_COUNT
    angles = 2.0 * np.pi / CHANNEL_COUNT * turns
    cosines = np.cos(angles).reshape(N, CH, NDLY).transpose(0, 2, 1)
    sines = np.sin(angles).reshape(N, CH, NDLY).transpose(0, 2, 1)
    ahead = np.concatenate(
        [np.concatenate([cosines, sines], axis=2), np.concatenate([-sines, cosines], axis=2)], axis=1
    )
    back = np.zeros((2 * NDLY, N, LANES))
    back[:NDLY, :, :CH] = sines.transpose(1, 0, 2)
    back[NDLY:, :, :CH] = cosines.transpose(1, 0, 2)
    return (ahead / CHANNEL_COUNT).astype(np.float32), back.reshape(2 * NDLY, N * LANES).astype(np.float32)


def kernel(
    vis_hbm, ants_hbm, gid_hbm, sky_hbm, start_hbm, coords_hbm, ahead_hbm, back_hbm,
    gains_out, cal_out, chi_out,
    vis, ants, gid, sky, start, coords, ahead, back,
    hot, grp_hot, hot_t, grp_hot_t, rows_a, rows_b, pair, gain, gain2, acc_grp, unique, unique2, acc_sum, acc_ant, rs_buf,
    ratio, part, coef_buf, model_t, model_band, square, vec_acc, vec_t, chi_acc,
    band_send_buf, band_buf, tot_buf,
    load_sem, rs_send, rs_recv, ag_send, ag_recv, mod_send, mod_recv, cr_send, cr_recv,
    band_send, band_recv, tot_send, tot_recv,
):
    me = lax.axis_index("grp")
    band = lax.axis_index("chan")
    i_own = lax.rem(me, 5) != 0
    my_unit = me - 1 - me // 5

    def others(body):
        for r in range(1, N):
            body(r)

    def grp_other(r):
        dx, dy = GRP_STEPS[r - 1]
        x = me // 4
        return lax.rem(x + dx, 4) * 4 + lax.rem(me - 4 * x + dy, 4)

    def chan_other(r):
        dz, core = CHAN_STEPS[r - 1]
        z = band // 2
        return lax.rem(z + dz, 8) * 2 + lax.rem(band - 2 * z + core, 2)

    loads = [
        pltpu.make_async_copy(ants_hbm, ants, load_sem.at[0]),
        pltpu.make_async_copy(gid_hbm, gid, load_sem.at[1]),
        pltpu.make_async_copy(coords_hbm, coords, load_sem.at[2]),
        pltpu.make_async_copy(start_hbm, start, load_sem.at[3]),
        pltpu.make_async_copy(vis_hbm, vis, load_sem.at[4]),
        pltpu.make_async_copy(sky_hbm, sky, load_sem.at[5]),
        pltpu.make_async_copy(ahead_hbm.at[band], ahead, load_sem.at[6]),
        pltpu.make_async_copy(back_hbm, back, load_sem.at[7]),
    ]
    for load in loads:
        load.start()

    barrier = pltpu.get_barrier_semaphore()

    def greet(r):
        pl.semaphore_signal(barrier, inc=1, device_id=(grp_other(r), band), device_id_type=MESH)
        pl.semaphore_signal(barrier, inc=1, device_id=(me, chan_other(r)), device_id_type=MESH)

    others(greet)

    loads[0].wait()
    loads[1].wait()
    loads[2].wait()
    vec_acc[...] = jnp.zeros_like(vec_acc)
    gain[:, :, ANT_PAD - LANES:] = jnp.zeros((2, CH, LANES), f32)
    gain[0, :8, :] = jnp.zeros((8, ANT_PAD), f32)
    gain[0, 0:2, :ANT] = coords[...]
    places = two_parts(gain[0, :8, :])

    def build(t, carry):
        cols = pl.ds(pl.multiple_of(t * TILE, TILE), TILE)
        ant_ids = lax.broadcasted_iota(jnp.int32, (ANT_PAD, TILE), 0)
        grp_ids = lax.broadcasted_iota(jnp.int32, (GRP, TILE), 0)
        p_hot = jnp.where(ant_ids == ants[0:1, cols], 1.0, 0.0).astype(bf16)
        q_hot = jnp.where(ant_ids == ants[1:2, cols], 1.0, 0.0).astype(bf16)
        g_hot = jnp.where(grp_ids == gid[0:1, cols], 1.0, 0.0).astype(bf16)
        hot[t, :, :TILE] = p_hot
        hot[t, :, TILE:] = q_hot
        grp_hot[t] = g_hot
        here = pl.multiple_of(2 * t * TILE, TILE)
        hot_t[pl.ds(here, TILE), :] = p_hot.T
        hot_t[pl.ds(here + TILE, TILE), :] = q_hot.T
        grp_hot_t[cols, :] = g_hot.T
        place = joined(dot(places, p_hot - q_hot))
        row = lax.broadcasted_iota(jnp.int32, place.shape, 0)
        place = jnp.where(row == 2, 1.0, place)
        vec_acc[...] += joined(dot_last(two_parts(place), g_hot))
        return carry

    lax.fori_loop(0, STEPS, build, 0, unroll=STEPS)

    loads[3].wait()
    gain[:, :, :ANT] = start[...]
    loads[4].wait()

    def rows_of(chunk):
        return pl.ds(pl.multiple_of(chunk * CHK, CHK), CHK)

    def group_fit(chunk):
        mine = rows_of(chunk)
        gain2[...] = two_parts(gain[:, mine, :].reshape(2 * CHK, ANT_PAD))

        for t in range(STEPS):
            cols = slice(t * TILE, (t + 1) * TILE)
            pq = joined(dot(gain2[...], hot[t]))
            pair[t] = pq
            a, b = pq[:CHK, :TILE], pq[CHK:, :TILE]
            c, d = pq[:CHK, TILE:], pq[CHK:, TILE:]
            x, y = vis[0, mine, cols], vis[1, mine, cols]
            wr = a * c + b * d
            wi = b * c - a * d
            rows = jnp.concatenate([x * wr + y * wi, y * wr - x * wi, wr * wr + wi * wi], axis=0)
            rows_a[:, cols] = two_parts(rows)
            if (t + 1) % SPAN == 0:
                part_cols = slice((t + 1 - SPAN) * TILE, (t + 1) * TILE)
                acc_grp[...] = dot(rows_a[:, part_cols], grp_hot_t[part_cols, :])

        sums = joined(acc_grp[...])
        scale = 1.0 / (sums[2 * CHK:] + RIDGE)
        ur, ui = sums[:CHK] * scale, sums[CHK:2 * CHK] * scale
        unique[0, mine, :] = ur
        unique[1, mine, :] = ui
        unique2[...] = two_parts(jnp.concatenate([ur, ui], axis=0))

    def antenna_sums(chunk):
        mine = rows_of(chunk)

        for t in range(STEPS):
            cols = slice(t * TILE, (t + 1) * TILE)
            uu = joined(dot(unique2[...], grp_hot[t]))
            s, v = uu[:CHK], uu[CHK:]
            pq = pair[t]
            a, b = pq[:CHK, :TILE], pq[CHK:, :TILE]
            c, d = pq[:CHK, TILE:], pq[CHK:, TILE:]
            x, y = vis[0, mine, cols], vis[1, mine, cols]
            zr = s * x + v * y
            zi = s * y - v * x
            size = s * s + v * v
            for_p = jnp.concatenate([c * zr - d * zi, c * zi + d * zr, size * (c * c + d * d)], axis=0)
            for_q = jnp.concatenate([a * zr + b * zi, b * zr - a * zi, size * (a * a + b * b)], axis=0)
            rows_b[:, 2 * t * TILE:(2 * t + 1) * TILE] = two_parts(for_p)
            rows_b[:, (2 * t + 1) * TILE:(2 * t + 2) * TILE] = two_parts(for_q)
            if (t + 1) % SPAN == 0:
                part_cols = slice(2 * (t + 1 - SPAN) * TILE, 2 * (t + 1) * TILE)
                acc_sum[...] = dot(rows_b[:, part_cols], hot_t[part_cols, :])

        acc_ant[chunk] = joined(acc_sum[...]).reshape(3, CHK, ANT_PAD)

    def misfit(chunk):
        mine = rows_of(chunk)
        chi_acc[mine, :] = jnp.zeros((CHK, LANES), f32)

        def step(t, carry):
            cols = pl.ds(pl.multiple_of(t * TILE, TILE), TILE)
            uu = joined(dot(unique2[...], grp_hot[t]))
            s, v = uu[:CHK], uu[CHK:]
            pq = pair[t]
            a, b = pq[:CHK, :TILE], pq[CHK:, :TILE]
            c, d = pq[:CHK, TILE:], pq[CHK:, TILE:]
            wr = a * c + b * d
            wi = b * c - a * d
            er = vis[0, mine, cols] - (wr * s - wi * v)
            ei = vis[1, mine, cols] - (wr * v + wi * s)
            e = er * er + ei * ei
            chi_acc[mine, :] += e[:, :LANES] + e[:, LANES:]
            return carry

        lax.fori_loop(0, STEPS, step, 0, unroll=STEPS)

    def place_of(unit):
        across = ANT_PAD // LANES
        tile = unit // across
        lanes = pl.ds(pl.multiple_of((unit - tile * across) * LANES, LANES), LANES)
        return tile * 8, lanes

    def rs_copy(chunk, unit):
        row, lanes = place_of(unit)
        return pltpu.make_async_remote_copy(
            src_ref=acc_ant.at[chunk, :, pl.ds(pl.multiple_of(row, 8), 8), lanes],
            dst_ref=rs_buf.at[chunk, me],
            send_sem=rs_send.at[chunk, unit], recv_sem=rs_recv.at[chunk, me],
            device_id=(owner_of(unit), band), device_id_type=MESH)

    def rs_arrival(chunk, source):
        return pltpu.make_async_remote_copy(
            src_ref=rs_buf.at[chunk, source], dst_ref=rs_buf.at[chunk, source],
            send_sem=rs_send.at[chunk, 0], recv_sem=rs_recv.at[chunk, source],
            device_id=(source, band), device_id_type=MESH)

    def ag_copy(chunk, unit, other):
        row, lanes = place_of(unit)
        block = gain.at[:, pl.ds(pl.multiple_of(chunk * CHK + row, 8), 8), lanes]
        return pltpu.make_async_remote_copy(
            src_ref=block, dst_ref=block,
            send_sem=ag_send.at[chunk, other], recv_sem=ag_recv.at[chunk, unit],
            device_id=(other, band), device_id_type=MESH)

    def units(body):
        def one(r):
            other = grp_other(r)

            @pl.when(lax.rem(other, 5) != 0)
            def _():
                body(other - 1 - other // 5)

        others(one)

    def send_sums(chunk):
        units(lambda unit: rs_copy(chunk, unit).start())

    def update_gains(chunk):
        @pl.when(i_own)
        def _():
            row, lanes = place_of(my_unit)
            rs_buf[chunk, me] = acc_ant[chunk, :, pl.ds(pl.multiple_of(row, 8), 8), lanes]
            others(lambda r: rs_arrival(chunk, grp_other(r)).wait_recv())
            total = rs_buf[chunk, 0]
            for source in range(1, N):
                total = total + rs_buf[chunk, source]
            share = 0.5 / (total[2] + RIDGE)
            here = pl.ds(pl.multiple_of(chunk * CHK + row, 8), 8)
            gain[0, here, lanes] = 0.5 * gain[0, here, lanes] + total[0] * share
            gain[1, here, lanes] = 0.5 * gain[1, here, lanes] + total[1] * share
            others(lambda r: ag_copy(chunk, my_unit, grp_other(r)).start())

    def await_gains(chunk):
        units(lambda unit: ag_copy(chunk, unit, owner_of(unit)).wait_recv())
        units(lambda unit: rs_copy(chunk, unit).wait_send())

        @pl.when(i_own)
        def _():
            others(lambda r: ag_copy(chunk, my_unit, grp_other(r)).wait_send())

    def mod_copy(source, other):
        return pltpu.make_async_remote_copy(
            src_ref=model_t.at[pl.ds(pl.multiple_of(other * OWN, OWN), OWN), :],
            dst_ref=model_band.at[:, pl.ds(pl.multiple_of(source * LANES, LANES), LANES)],
            send_sem=mod_send.at[other], recv_sem=mod_recv.at[source],
            device_id=(me, other), device_id_type=MESH)

    def iteration(s, carry):
        chunk = lax.rem(s, CHUNKS)

        @pl.when(s >= CHUNKS)
        def _():
            await_gains(chunk)

        group_fit(chunk)
        antenna_sums(chunk)

        @pl.when(s == 0)
        def _():
            pl.semaphore_wait(barrier, 2 * (N - 1))

        send_sums(chunk)

        @pl.when(s >= 1)
        def _():
            update_gains(lax.rem(s + CHUNKS - 1, CHUNKS))

        @pl.when(s == 0)
        def _():
            loads[5].wait()
            model = sky[0] * sky[0] + sky[1] * sky[1]
            square[CH:, :] = jnp.zeros((LANES - CH, LANES), f32)
            square[:CH, :] = model
            model_t[...] = square[...].T
            own_rows = pl.ds(pl.multiple_of(band * OWN, OWN), OWN)
            own_lanes = pl.ds(pl.multiple_of(band * LANES, LANES), LANES)
            model_band[:, own_lanes] = model_t[own_rows, :]
            others(lambda r: mod_copy(band, chan_other(r)).start())

        return carry

    lax.fori_loop(0, ITERS * CHUNKS, iteration, 0)

    def last(chunk, carry):
        await_gains(chunk)
        group_fit(chunk)

        @pl.when(chunk == 0)
        def _():
            update_gains(CHUNKS - 1)

        misfit(chunk)
        return carry

    lax.fori_loop(0, CHUNKS, last, 0)

    ur, ui = unique[0], unique[1]
    sr, si = sky[0], sky[1]
    ratio[:CH, :] = ur * sr + ui * si
    ratio[CH:, :] = ui * sr - ur * si
    loads[6].wait()
    part[...] = exact_dot(ahead[...], ratio[...]).T

    def cr_copy(source, other):
        return pltpu.make_async_remote_copy(
            src_ref=part.at[pl.ds(pl.multiple_of(other * OWN, OWN), OWN), :], dst_ref=coef_buf.at[source],
            send_sem=cr_send.at[other], recv_sem=cr_recv.at[source],
            device_id=(me, other), device_id_type=MESH)

    others(lambda r: cr_copy(band, chan_other(r)).start())
    coef_buf[band] = part[pl.ds(pl.multiple_of(band * OWN, OWN), OWN), :]

    gains_out[...] = gain[:, :, :ANT]
    east = vec_acc[0:1, :] / vec_acc[2:3, :]
    north = vec_acc[1:2, :] / vec_acc[2:3, :]
    square[...] = jnp.zeros_like(square)
    square[0:1, :] = east
    square[1:2, :] = north
    vec_t[...] = square[...].T
    model = sr * sr + si * si
    squared = model * model
    fields = [
        ur * ur + ui * ui, model, squared * (east * east), squared * (east * north),
        squared * (north * north), chi_acc[...],
    ]
    lane = lax.broadcasted_iota(jnp.int32, (CH, LANES), 1)
    table = jnp.zeros((CH, LANES), f32)
    for place, field in enumerate(fields):
        table = jnp.where(lane == place, jnp.sum(field, axis=1, keepdims=True), table)
    square[CH:, :] = jnp.zeros((LANES - CH, LANES), f32)
    square[:CH, :] = table
    local = square[...].T[:8, :]

    channel = band * CH + lax.broadcasted_iota(jnp.int32, (1, LANES), 1)
    frequency = 1.0 + channel.astype(f32) * (1.0 / CHANNEL_COUNT)
    squares = frequency * frequency
    slope_parts = squares * local[2:5]
    at = lax.broadcasted_iota(jnp.int32, (1, N * LANES), 1)
    band_channel = (at // LANES) * CH + lax.rem(at, LANES)
    band_frequency = 1.0 + band_channel.astype(f32) * (1.0 / CHANNEL_COUNT)
    my_groups = vec_t[pl.ds(pl.multiple_of(band * OWN, OWN), OWN), :]

    loads[7].wait()
    others(lambda r: mod_copy(chan_other(r), band).wait_recv())
    others(lambda r: mod_copy(band, chan_other(r)).wait_send())
    weights_east = model_band[...] * my_groups[:, 0:1]
    weights_north = model_band[...] * my_groups[:, 1:2]

    others(lambda r: cr_copy(chan_other(r), band).wait_recv())
    coef = coef_buf[0]
    for source in range(1, N):
        coef = coef + coef_buf[source]
    phases = exact_dot(coef, back[...])
    right_east = jnp.sum(weights_east * phases, axis=0, keepdims=True)
    right_north = jnp.sum(weights_north * phases, axis=0, keepdims=True)
    slope_east = jnp.sum(band_frequency * right_east, axis=1, keepdims=True)
    slope_north = jnp.sum(band_frequency * right_north, axis=1, keepdims=True)
    first_lane = lax.broadcasted_iota(jnp.int32, (1, LANES), 1) == 0
    slope_rows = jnp.concatenate(
        [jnp.where(first_lane, slope_east, 0.0), jnp.where(first_lane, slope_north, 0.0),
         slope_parts, jnp.zeros((1, LANES), f32)], axis=0)
    for other in range(N):
        lanes = slice(other * LANES, (other + 1) * LANES)
        band_send_buf[other] = jnp.concatenate([right_east[:, lanes], right_north[:, lanes], slope_rows], axis=0)

    def band_copy(source, other):
        return pltpu.make_async_remote_copy(
            src_ref=band_send_buf.at[other], dst_ref=band_buf.at[source],
            send_sem=band_send.at[other], recv_sem=band_recv.at[source],
            device_id=(me, other), device_id_type=MESH)

    others(lambda r: band_copy(band, chan_other(r)).start())
    band_buf[band] = band_send_buf[band]
    others(lambda r: cr_copy(band, chan_other(r)).wait_send())
    others(lambda r: band_copy(chan_other(r), band).wait_recv())
    sums = band_buf[0]
    for source in range(1, N):
        sums = sums + band_buf[source]

    tot_buf[me] = jnp.concatenate(
        [local[0:5], sums[0:2], local[5:6], sums[2:7], jnp.zeros((3, LANES), f32)], axis=0)

    def tot_copy(source, other):
        return pltpu.make_async_remote_copy(
            src_ref=tot_buf.at[source], dst_ref=tot_buf.at[source],
            send_sem=tot_send.at[other], recv_sem=tot_recv.at[source],
            device_id=(other, band), device_id_type=MESH)

    others(lambda r: tot_copy(me, grp_other(r)).start())
    others(lambda r: band_copy(band, chan_other(r)).wait_send())
    others(lambda r: tot_copy(grp_other(r), me).wait_recv())
    totals = tot_buf[0]
    for source in range(1, N):
        totals = totals + tot_buf[source]
    others(lambda r: tot_copy(me, grp_other(r)).wait_send())
    chi_out[...] = totals[7:8, :CH]

    terms = jnp.sum(totals[8:16], axis=1, keepdims=True)
    slope_east, slope_north = solve_pair(
        terms[2:3], terms[3:4], terms[4:5], terms[0:1], terms[1:2])
    tilt_east, tilt_north = solve_pair(
        totals[2:3], totals[3:4], totals[4:5], totals[5:6], totals[6:7])
    tilt_east = tilt_east - frequency * slope_east
    tilt_north = tilt_north - frequency * slope_north
    amplitude = jnp.sqrt((totals[0:1] + EPSILON) / (totals[1:2] + EPSILON))
    square[0:8, :] = jnp.concatenate(
        [frequency, tilt_east, tilt_north, 1.0 / amplitude, jnp.zeros((4, LANES), f32)], axis=0)
    columns = square[...].T[:CH, :]
    along = slope_east * east + slope_north * north
    turn = columns[:, 0:1] * along + columns[:, 1:2] * east + columns[:, 2:3] * north
    rotation_cos = jnp.cos(turn) * columns[:, 3:4]
    rotation_sin = jnp.sin(turn) * columns[:, 3:4]
    cal_out[0] = ur * rotation_cos + ui * rotation_sin
    cal_out[1] = ui * rotation_cos - ur * rotation_sin


def per_device(ahead, back, vis, ants, gid, sky, start, coords):
    vmem = pl.BlockSpec(memory_space=pltpu.VMEM)
    hbm = pl.BlockSpec(memory_space=pltpu.HBM)
    dma = pltpu.SemaphoreType.DMA
    gains, cal, chi = pl.pallas_call(
        kernel,
        out_shape=(
            jax.ShapeDtypeStruct((2, CH, ANT), f32),
            jax.ShapeDtypeStruct((2, CH, GRP), f32),
            jax.ShapeDtypeStruct((1, CH), f32),
        ),
        in_specs=[hbm] * 8,
        out_specs=(vmem, vmem, vmem),
        scratch_shapes=[
            pltpu.VMEM((2, CH, BL), f32),
            pltpu.VMEM((2, BL), jnp.int32),
            pltpu.VMEM((1, BL), jnp.int32),
            pltpu.VMEM((2, CH, GRP), f32),
            pltpu.VMEM((2, CH, ANT), f32),
            pltpu.VMEM((2, ANT), f32),
            pltpu.VMEM((2 * NDLY, 2 * CH), f32),
            pltpu.VMEM((2 * NDLY, N * LANES), f32),
            pltpu.VMEM((STEPS, ANT_PAD, 2 * TILE), bf16),
            pltpu.VMEM((STEPS, GRP, TILE), bf16),
            pltpu.VMEM((2 * BL, ANT_PAD), bf16),
            pltpu.VMEM((BL, GRP), bf16),
            pltpu.VMEM((6 * CHK, BL), bf16),
            pltpu.VMEM((6 * CHK, 2 * BL), bf16),
            pltpu.VMEM((STEPS, 2 * CHK, 2 * TILE), f32),
            pltpu.VMEM((2, CH, ANT_PAD), f32),
            pltpu.VMEM((4 * CHK, ANT_PAD), bf16),
            pltpu.VMEM((6 * CHK, GRP), f32),
            pltpu.VMEM((2, CH, GRP), f32),
            pltpu.VMEM((4 * CHK, GRP), bf16),
            pltpu.VMEM((6 * CHK, ANT_PAD), f32),
            pltpu.VMEM((CHUNKS, 3, CHK, ANT_PAD), f32),
            pltpu.VMEM((CHUNKS, N, 3, 8, LANES), f32),
            pltpu.VMEM((2 * CH, GRP), f32),
            pltpu.VMEM((GRP, 2 * NDLY), f32),
            pltpu.VMEM((N, OWN, 2 * NDLY), f32),
            pltpu.VMEM((GRP, LANES), f32),
            pltpu.VMEM((OWN, N * LANES), f32),
            pltpu.VMEM((LANES, LANES), f32),
            pltpu.VMEM((8, GRP), f32),
            pltpu.VMEM((GRP, LANES), f32),
            pltpu.VMEM((CH, LANES), f32),
            pltpu.VMEM((N, 8, LANES), f32),
            pltpu.VMEM((N, 8, LANES), f32),
            pltpu.VMEM((N, 16, LANES), f32),
            dma((8,)),
            dma((CHUNKS, UNITS)), dma((CHUNKS, N)), dma((CHUNKS, N)), dma((CHUNKS, UNITS)),
        ] + [dma((N,))] * 8,
        compiler_params=pltpu.CompilerParams(
            collective_id=0, has_side_effects=True, vmem_limit_bytes=60 * 1024 * 1024),
        cost_estimate=pl.CostEstimate(flops=20_000_000_000, bytes_accessed=4_000_000, transcendentals=0),
    )(vis, ants, gid, sky, start, coords, ahead, back)
    return gains, cal, chi.reshape(CH)


def solution(mesh):
    ahead, back = delay_tables()

    def program(vis, ants, gid, sky, start, coords):
        return jax.shard_map(
            functools.partial(per_device, ahead, back),
            mesh=mesh,
            in_specs=(
                P(None, "chan", "grp"),
                P(None, "grp"),
                P("grp", None),
                P(None, "chan", "grp"),
                P(None, "chan", None),
                P(),
            ),
            out_specs=(P(None, "chan", None), P(None, "chan", "grp"), P("chan")),
            check_vma=False,
        )(vis, ants, gid, sky, start, coords)

    return program
```

```python
import functools

import jax
import jax.numpy as jnp
import numpy as np
from jax import lax
from jax.experimental import pallas as pl
from jax.experimental.pallas import tpu as pltpu
from jax.sharding import PartitionSpec as P

CHANNEL_COUNT = 1536
NDLY = 64
ITERS = 4
RIDGE = 0.5
EPSILON = 1e-06

N = 16
ANT = 350
ANT_PAD = 384
CH = 96
CHUNKS = 3
CHK = CH // CHUNKS
BL = 2048
GRP = 128
TILE = 256
STEPS = BL // TILE
SPAN = 8
OWN = GRP // N
LANES = 128
UNITS = (CHK // 8) * (ANT_PAD // LANES)

GRP_STEPS = sorted(
    ((dx, dy) for dx in range(4) for dy in range(4) if dx or dy),
    key=lambda step: -min(step[0], 4 - step[0]) - min(step[1], 4 - step[1]))
CHAN_STEPS = sorted(
    ((dz, core) for dz in range(8) for core in range(2) if dz or core),
    key=lambda step: -2 * min(step[0], 8 - step[0]) - step[1])

MESH = pl.DeviceIdType.MESH
f32 = jnp.float32
bf16 = jnp.bfloat16


def owner_of(unit):
    return unit + 1 + unit // 4


def two_parts(number):
    first = number.astype(bf16)
    rest = (number - first.astype(f32)).astype(bf16)
    return jnp.concatenate([first, rest], axis=0)


def joined(parts):
    half = parts.shape[0] // 2
    return parts[:half] + parts[half:]


def dot(left, right):
    return jnp.dot(left, right, preferred_element_type=f32)


def dot_last(left, right):
    return lax.dot_general(left, right, (((1,), (1,)), ((), ())), preferred_element_type=f32)


def solve_pair(entry_xx, entry_xy, entry_yy, right_x, right_y):
    ridge_shift = 0.001 * (entry_xx + entry_yy) + EPSILON
    diag_first = entry_xx + ridge_shift
    diag_second = entry_yy + ridge_shift
    determinant = diag_first * diag_second - entry_xy * entry_xy
    return (
        (diag_second * right_x - entry_xy * right_y) / determinant,
        (diag_first * right_y - entry_xy * right_x) / determinant,
    )


def delay_tables():
    channel_ids = np.arange(CHANNEL_COUNT)
    turns = (channel_ids[:, None] * (np.arange(NDLY)[None, :] - NDLY // 2)) % CHANNEL_COUNT
    angles = 2.0 * np.pi / CHANNEL_COUNT * turns
    cosines = np.cos(angles).reshape(N, CH, NDLY).transpose(0, 2, 1)
    sines = np.sin(angles).reshape(N, CH, NDLY).transpose(0, 2, 1)
    ahead = np.concatenate(
        [np.concatenate([cosines, sines], axis=2), np.concatenate([-sines, cosines], axis=2)], axis=1
    )
    back = np.zeros((2 * NDLY, N, LANES))
    back[:NDLY, :, :CH] = sines.transpose(1, 0, 2)
    back[NDLY:, :, :CH] = cosines.transpose(1, 0, 2)
    ahead = ahead / CHANNEL_COUNT
    back = back.reshape(2 * NDLY, N * LANES)
    ahead_1, back_1 = ahead.astype(bf16), back.astype(bf16)
    ahead_2 = (ahead - ahead_1.astype(np.float64)).astype(bf16)
    back_2 = (back - back_1.astype(np.float64)).astype(bf16)
    ahead = np.concatenate(
        [np.concatenate([ahead_1, ahead_1], axis=2), np.concatenate([ahead_2, ahead_2], axis=2)], axis=1)
    return ahead, np.concatenate([back_1, back_2], axis=0)


def kernel(
    vis_hbm, ants_hbm, gid_hbm, sky_hbm, start_hbm, coords_hbm, ahead_hbm, back_hbm,
    gains_out, cal_out, chi_out,
    vis, ants, gid, sky, start, coords, ahead, back,
    hot, grp_hot, hot_t, grp_hot_t, rows_a, rows_b, pair, gain, gain2, acc_grp, unique, unique2, acc_sum, acc_ant, rs_buf,
    ratio, part, coef_buf, model_t, model_band, square, vec_acc, vec_t, chi_acc,
    band_send_buf, band_buf, tot_buf,
    load_sem, rs_send, rs_recv, ag_send, ag_recv, mod_send, mod_recv, cr_send, cr_recv,
    band_send, band_recv, tot_send, tot_recv,
):
    me = lax.axis_index("grp")
    band = lax.axis_index("chan")
    i_own = lax.rem(me, 5) != 0
    my_unit = me - 1 - me // 5

    def others(body):
        for r in range(1, N):
            body(r)

    def grp_other(r):
        dx, dy = GRP_STEPS[r - 1]
        x = me // 4
        return lax.rem(x + dx, 4) * 4 + lax.rem(me - 4 * x + dy, 4)

    def chan_other(r):
        dz, core = CHAN_STEPS[r - 1]
        z = band // 2
        return lax.rem(z + dz, 8) * 2 + lax.rem(band - 2 * z + core, 2)

    loads = [
        pltpu.make_async_copy(ants_hbm, ants, load_sem.at[0]),
        pltpu.make_async_copy(gid_hbm, gid, load_sem.at[1]),
        pltpu.make_async_copy(coords_hbm, coords, load_sem.at[2]),
        pltpu.make_async_copy(start_hbm, start, load_sem.at[3]),
        pltpu.make_async_copy(vis_hbm.at[:, 0:CHK], vis.at[:, 0:CHK], load_sem.at[4]),
        pltpu.make_async_copy(sky_hbm, sky, load_sem.at[5]),
        pltpu.make_async_copy(ahead_hbm.at[band], ahead, load_sem.at[6]),
        pltpu.make_async_copy(back_hbm, back, load_sem.at[7]),
    ] + [
        pltpu.make_async_copy(
            vis_hbm.at[:, c * CHK:(c + 1) * CHK], vis.at[:, c * CHK:(c + 1) * CHK], load_sem.at[7 + c])
        for c in range(1, CHUNKS)
    ]
    for load in loads:
        load.start()

    barrier = pltpu.get_barrier_semaphore()

    def greet(r):
        pl.semaphore_signal(barrier, inc=1, device_id=(grp_other(r), band), device_id_type=MESH)
        pl.semaphore_signal(barrier, inc=1, device_id=(me, chan_other(r)), device_id_type=MESH)

    others(greet)

    loads[0].wait()
    loads[1].wait()
    loads[2].wait()
    vec_acc[...] = jnp.zeros_like(vec_acc)
    gain[:, :, ANT_PAD - LANES:] = jnp.zeros((2, CH, LANES), f32)
    gain[0, :8, :] = jnp.zeros((8, ANT_PAD), f32)
    gain[0, 0:2, :ANT] = coords[...]
    places = two_parts(gain[0, :8, :])

    def build(t, carry):
        cols = pl.ds(pl.multiple_of(t * TILE, TILE), TILE)
        ant_ids = lax.broadcasted_iota(jnp.int32, (ANT_PAD, TILE), 0)
        grp_ids = lax.broadcasted_iota(jnp.int32, (GRP, TILE), 0)
        p_hot = jnp.where(ant_ids == ants[0:1, cols], 1.0, 0.0).astype(bf16)
        q_hot = jnp.where(ant_ids == ants[1:2, cols], 1.0, 0.0).astype(bf16)
        g_hot = jnp.where(grp_ids == gid[0:1, cols], 1.0, 0.0).astype(bf16)
        hot[t, :, :TILE] = p_hot
        hot[t, :, TILE:] = q_hot
        grp_hot[t] = g_hot
        here = pl.multiple_of(2 * t * TILE, TILE)
        hot_t[pl.ds(here, TILE), :] = p_hot.T
        hot_t[pl.ds(here + TILE, TILE), :] = q_hot.T
        grp_hot_t[cols, :] = g_hot.T
        place = joined(dot(places, p_hot - q_hot))
        row = lax.broadcasted_iota(jnp.int32, place.shape, 0)
        place = jnp.where(row == 2, 1.0, place)
        vec_acc[...] += joined(dot_last(two_parts(place), g_hot))
        return carry

    lax.fori_loop(0, STEPS, build, 0, unroll=STEPS)

    loads[3].wait()
    gain[:, :, :ANT] = start[...]
    loads[4].wait()

    def rows_of(chunk):
        return pl.ds(pl.multiple_of(chunk * CHK, CHK), CHK)

    def group_fit(chunk):
        mine = rows_of(chunk)
        gain2[...] = two_parts(gain[:, mine, :].reshape(2 * CHK, ANT_PAD))

        for t in range(STEPS):
            cols = slice(t * TILE, (t + 1) * TILE)
            pq = joined(dot(gain2[...], hot[t]))
            pair[t] = pq
            a, b = pq[:CHK, :TILE], pq[CHK:, :TILE]
            c, d = pq[:CHK, TILE:], pq[CHK:, TILE:]
            x, y = vis[0, mine, cols], vis[1, mine, cols]
            wr = a * c + b * d
            wi = b * c - a * d
            rows = jnp.concatenate([x * wr + y * wi, y * wr - x * wi, wr * wr + wi * wi], axis=0)
            rows_a[:, cols] = two_parts(rows)
            if (t + 1) % SPAN == 0:
                part_cols = slice((t + 1 - SPAN) * TILE, (t + 1) * TILE)
                acc_grp[...] = dot(rows_a[:, part_cols], grp_hot_t[part_cols, :])

        sums = joined(acc_grp[...])
        scale = 1.0 / (sums[2 * CHK:] + RIDGE)
        ur, ui = sums[:CHK] * scale, sums[CHK:2 * CHK] * scale
        unique[0, mine, :] = ur
        unique[1, mine, :] = ui
        unique2[...] = two_parts(jnp.concatenate([ur, ui], axis=0))

    def antenna_sums(chunk):
        mine = rows_of(chunk)

        for t in range(STEPS):
            cols = slice(t * TILE, (t + 1) * TILE)
            uu = joined(dot(unique2[...], grp_hot[t]))
            s, v = uu[:CHK], uu[CHK:]
            pq = pair[t]
            a, b = pq[:CHK, :TILE], pq[CHK:, :TILE]
            c, d = pq[:CHK, TILE:], pq[CHK:, TILE:]
            x, y = vis[0, mine, cols], vis[1, mine, cols]
            zr = s * x + v * y
            zi = s * y - v * x
            size = s * s + v * v
            for_p = jnp.concatenate([c * zr - d * zi, c * zi + d * zr, size * (c * c + d * d)], axis=0)
            for_q = jnp.concatenate([a * zr + b * zi, b * zr - a * zi, size * (a * a + b * b)], axis=0)
            rows_b[:, 2 * t * TILE:(2 * t + 1) * TILE] = two_parts(for_p)
            rows_b[:, (2 * t + 1) * TILE:(2 * t + 2) * TILE] = two_parts(for_q)
            if (t + 1) % SPAN == 0:
                part_cols = slice(2 * (t + 1 - SPAN) * TILE, 2 * (t + 1) * TILE)
                acc_sum[...] = dot(rows_b[:, part_cols], hot_t[part_cols, :])

        acc_ant[chunk] = joined(acc_sum[...]).reshape(3, CHK, ANT_PAD)

    def misfit(chunk):
        mine = rows_of(chunk)
        chi_acc[mine, :] = jnp.zeros((CHK, LANES), f32)

        def step(t, carry):
            cols = pl.ds(pl.multiple_of(t * TILE, TILE), TILE)
            uu = joined(dot(unique2[...], grp_hot[t]))
            s, v = uu[:CHK], uu[CHK:]
            pq = pair[t]
            a, b = pq[:CHK, :TILE], pq[CHK:, :TILE]
            c, d = pq[:CHK, TILE:], pq[CHK:, TILE:]
            wr = a * c + b * d
            wi = b * c - a * d
            er = vis[0, mine, cols] - (wr * s - wi * v)
            ei = vis[1, mine, cols] - (wr * v + wi * s)
            e = er * er + ei * ei
            chi_acc[mine, :] += e[:, :LANES] + e[:, LANES:]
            return carry

        lax.fori_loop(0, STEPS, step, 0, unroll=STEPS)

    def place_of(unit):
        across = ANT_PAD // LANES
        tile = unit // across
        lanes = pl.ds(pl.multiple_of((unit - tile * across) * LANES, LANES), LANES)
        return tile * 8, lanes

    def rs_copy(chunk, unit):
        row, lanes = place_of(unit)
        return pltpu.make_async_remote_copy(
            src_ref=acc_ant.at[chunk, :, pl.ds(pl.multiple_of(row, 8), 8), lanes],
            dst_ref=rs_buf.at[chunk, me],
            send_sem=rs_send.at[chunk], recv_sem=rs_recv.at[chunk],
            device_id=(owner_of(unit), band), device_id_type=MESH)

    def arrivals(sem, shape):
        return pltpu.make_async_copy(shape, shape, sem)

    def ag_copy(chunk, unit, other):
        row, lanes = place_of(unit)
        block = gain.at[:, pl.ds(pl.multiple_of(chunk * CHK + row, 8), 8), lanes]
        return pltpu.make_async_remote_copy(
            src_ref=block, dst_ref=block,
            send_sem=ag_send.at[chunk], recv_sem=ag_recv.at[chunk],
            device_id=(other, band), device_id_type=MESH)

    def units(body):
        def one(r):
            other = grp_other(r)

            @pl.when(lax.rem(other, 5) != 0)
            def _():
                body(other - 1 - other // 5)

        others(one)

    def send_sums(chunk):
        units(lambda unit: rs_copy(chunk, unit).start())

    def update_gains(chunk):
        @pl.when(i_own)
        def _():
            row, lanes = place_of(my_unit)
            rs_buf[chunk, me] = acc_ant[chunk, :, pl.ds(pl.multiple_of(row, 8), 8), lanes]
            arrivals(rs_recv.at[chunk], rs_buf.at[chunk, 0:N - 1]).wait()
            total = rs_buf[chunk, 0]
            for source in range(1, N):
                total = total + rs_buf[chunk, source]
            share = 0.5 / (total[2] + RIDGE)
            here = pl.ds(pl.multiple_of(chunk * CHK + row, 8), 8)
            gain[0, here, lanes] = 0.5 * gain[0, here, lanes] + total[0] * share
            gain[1, here, lanes] = 0.5 * gain[1, here, lanes] + total[1] * share
            others(lambda r: ag_copy(chunk, my_unit, grp_other(r)).start())

    def by_place(body):
        @pl.when(i_own)
        def _():
            body(UNITS - 1)

        @pl.when(jnp.logical_not(i_own))
        def _():
            body(UNITS)

    def await_gains(chunk):
        by_place(lambda n: arrivals(ag_recv.at[chunk], rs_buf.at[chunk, 0:n, 0:2]).wait())

    def settle(chunk):
        by_place(lambda n: arrivals(rs_send.at[chunk], rs_buf.at[chunk, 0:n]).wait())

        @pl.when(i_own)
        def _():
            arrivals(ag_send.at[chunk], rs_buf.at[chunk, 0:N - 1, 0:2]).wait()

    def mod_copy(source, other):
        return pltpu.make_async_remote_copy(
            src_ref=model_t.at[pl.ds(pl.multiple_of(other * OWN, OWN), OWN), :],
            dst_ref=model_band.at[:, pl.ds(pl.multiple_of(source * LANES, LANES), LANES)],
            send_sem=mod_send.at[other], recv_sem=mod_recv.at[source],
            device_id=(me, other), device_id_type=MESH)

    def iteration(s, carry):
        chunk = lax.rem(s, CHUNKS)

        @pl.when(s >= CHUNKS)
        def _():
            await_gains(chunk)

        for c in range(1, CHUNKS):
            @pl.when(s == c)
            def _():
                loads[7 + c].wait()

        group_fit(chunk)

        @pl.when(s >= CHUNKS)
        def _():
            settle(chunk)

        antenna_sums(chunk)

        @pl.when(s == 0)
        def _():
            pl.semaphore_wait(barrier, 2 * (N - 1))

        send_sums(chunk)

        @pl.when(s == CHUNKS - 1)
        def _():
            loads[5].wait()
            model = sky[0] * sky[0] + sky[1] * sky[1]
            square[CH:, :] = jnp.zeros((LANES - CH, LANES), f32)
            square[:CH, :] = model
            model_t[...] = square[...].T
            own_rows = pl.ds(pl.multiple_of(band * OWN, OWN), OWN)
            own_lanes = pl.ds(pl.multiple_of(band * LANES, LANES), LANES)
            model_band[:, own_lanes] = model_t[own_rows, :]
            others(lambda r: mod_copy(band, chan_other(r)).start())

        @pl.when(s >= 1)
        def _():
            update_gains(lax.rem(s + CHUNKS - 1, CHUNKS))

        return carry

    lax.fori_loop(0, ITERS * CHUNKS, iteration, 0)

    def last(chunk, carry):
        await_gains(chunk)
        group_fit(chunk)

        settle(chunk)

        @pl.when(chunk == 0)
        def _():
            update_gains(CHUNKS - 1)

        @pl.when(chunk < CHUNKS - 1)
        def _():
            misfit(chunk)

        return carry

    lax.fori_loop(0, CHUNKS, last, 0)

    ur, ui = unique[0], unique[1]
    sr, si = sky[0], sky[1]
    ratio[:CH, :] = ur * sr + ui * si
    ratio[CH:, :] = ui * sr - ur * si
    loads[6].wait()
    part[...] = joined(dot(ahead[...], two_parts(ratio[...]))).T

    def cr_copy(source, other):
        return pltpu.make_async_remote_copy(
            src_ref=part.at[pl.ds(pl.multiple_of(other * OWN, OWN), OWN), :], dst_ref=coef_buf.at[source],
            send_sem=cr_send.at[other], recv_sem=cr_recv.at[source],
            device_id=(me, other), device_id_type=MESH)

    others(lambda r: cr_copy(band, chan_other(r)).start())
    coef_buf[band] = part[pl.ds(pl.multiple_of(band * OWN, OWN), OWN), :]
    misfit(CHUNKS - 1)

    gains_out[...] = gain[:, :, :ANT]
    east = vec_acc[0:1, :] / vec_acc[2:3, :]
    north = vec_acc[1:2, :] / vec_acc[2:3, :]
    square[...] = jnp.zeros_like(square)
    square[0:1, :] = east
    square[1:2, :] = north
    vec_t[...] = square[...].T
    model = sr * sr + si * si
    squared = model * model
    fields = [
        ur * ur + ui * ui, model, squared * (east * east), squared * (east * north),
        squared * (north * north), chi_acc[...],
    ]
    lane = lax.broadcasted_iota(jnp.int32, (CH, LANES), 1)
    table = jnp.zeros((CH, LANES), f32)
    for place, field in enumerate(fields):
        table = jnp.where(lane == place, jnp.sum(field, axis=1, keepdims=True), table)
    square[CH:, :] = jnp.zeros((LANES - CH, LANES), f32)
    square[:CH, :] = table
    local = square[...].T[:8, :]

    channel = band * CH + lax.broadcasted_iota(jnp.int32, (1, LANES), 1)
    frequency = 1.0 + channel.astype(f32) * (1.0 / CHANNEL_COUNT)
    squares = frequency * frequency
    slope_parts = squares * local[2:5]
    at = lax.broadcasted_iota(jnp.int32, (1, N * LANES), 1)
    band_channel = (at // LANES) * CH + lax.rem(at, LANES)
    band_frequency = 1.0 + band_channel.astype(f32) * (1.0 / CHANNEL_COUNT)
    my_groups = vec_t[pl.ds(pl.multiple_of(band * OWN, OWN), OWN), :]

    loads[7].wait()
    others(lambda r: mod_copy(chan_other(r), band).wait_recv())
    others(lambda r: mod_copy(band, chan_other(r)).wait_send())
    weights_east = model_band[...] * my_groups[:, 0:1]
    weights_north = model_band[...] * my_groups[:, 1:2]

    others(lambda r: cr_copy(chan_other(r), band).wait_recv())
    coef = coef_buf[0]
    for source in range(1, N):
        coef = coef + coef_buf[source]
    coef = two_parts(coef)
    phases = joined(dot(jnp.concatenate([coef, coef], axis=1), back[...]))
    right_east = jnp.sum(weights_east * phases, axis=0, keepdims=True)
    right_north = jnp.sum(weights_north * phases, axis=0, keepdims=True)
    slope_east = jnp.sum(band_frequency * right_east, axis=1, keepdims=True)
    slope_north = jnp.sum(band_frequency * right_north, axis=1, keepdims=True)
    first_lane = lax.broadcasted_iota(jnp.int32, (1, LANES), 1) == 0
    slope_rows = jnp.concatenate(
        [jnp.where(first_lane, slope_east, 0.0), jnp.where(first_lane, slope_north, 0.0),
         slope_parts, jnp.zeros((1, LANES), f32)], axis=0)
    for other in range(N):
        lanes = slice(other * LANES, (other + 1) * LANES)
        band_send_buf[other] = jnp.concatenate([right_east[:, lanes], right_north[:, lanes], slope_rows], axis=0)

    def band_copy(source, other):
        return pltpu.make_async_remote_copy(
            src_ref=band_send_buf.at[other], dst_ref=band_buf.at[source],
            send_sem=band_send.at[other], recv_sem=band_recv.at[source],
            device_id=(me, other), device_id_type=MESH)

    others(lambda r: band_copy(band, chan_other(r)).start())
    band_buf[band] = band_send_buf[band]
    others(lambda r: cr_copy(band, chan_other(r)).wait_send())
    others(lambda r: band_copy(chan_other(r), band).wait_recv())
    sums = band_buf[0]
    for source in range(1, N):
        sums = sums + band_buf[source]

    tot_buf[me] = jnp.concatenate(
        [local[0:5], sums[0:2], local[5:6], sums[2:7], jnp.zeros((3, LANES), f32)], axis=0)

    def tot_copy(source, other):
        return pltpu.make_async_remote_copy(
            src_ref=tot_buf.at[source], dst_ref=tot_buf.at[source],
            send_sem=tot_send.at[other], recv_sem=tot_recv.at[source],
            device_id=(other, band), device_id_type=MESH)

    others(lambda r: tot_copy(me, grp_other(r)).start())
    others(lambda r: band_copy(band, chan_other(r)).wait_send())
    others(lambda r: tot_copy(grp_other(r), me).wait_recv())
    totals = tot_buf[0]
    for source in range(1, N):
        totals = totals + tot_buf[source]
    others(lambda r: tot_copy(me, grp_other(r)).wait_send())
    chi_out[...] = totals[7:8, :CH]

    terms = jnp.sum(totals[8:16], axis=1, keepdims=True)
    slope_east, slope_north = solve_pair(
        terms[2:3], terms[3:4], terms[4:5], terms[0:1], terms[1:2])
    tilt_east, tilt_north = solve_pair(
        totals[2:3], totals[3:4], totals[4:5], totals[5:6], totals[6:7])
    tilt_east = tilt_east - frequency * slope_east
    tilt_north = tilt_north - frequency * slope_north
    amplitude = jnp.sqrt((totals[0:1] + EPSILON) / (totals[1:2] + EPSILON))
    square[0:8, :] = jnp.concatenate(
        [frequency, tilt_east, tilt_north, 1.0 / amplitude, jnp.zeros((4, LANES), f32)], axis=0)
    columns = square[...].T[:CH, :]
    along = slope_east * east + slope_north * north
    turn = columns[:, 0:1] * along + columns[:, 1:2] * east + columns[:, 2:3] * north
    rotation_cos = jnp.cos(turn) * columns[:, 3:4]
    rotation_sin = jnp.sin(turn) * columns[:, 3:4]
    cal_out[0] = ur * rotation_cos + ui * rotation_sin
    cal_out[1] = ui * rotation_cos - ur * rotation_sin


def per_device(ahead, back, vis, ants, gid, sky, start, coords):
    vmem = pl.BlockSpec(memory_space=pltpu.VMEM)
    hbm = pl.BlockSpec(memory_space=pltpu.HBM)
    dma = pltpu.SemaphoreType.DMA
    gains, cal, chi = pl.pallas_call(
        kernel,
        out_shape=(
            jax.ShapeDtypeStruct((2, CH, ANT), f32),
            jax.ShapeDtypeStruct((2, CH, GRP), f32),
            jax.ShapeDtypeStruct((1, CH), f32),
        ),
        in_specs=[hbm] * 8,
        out_specs=(vmem, vmem, vmem),
        scratch_shapes=[
            pltpu.VMEM((2, CH, BL), f32),
            pltpu.VMEM((2, BL), jnp.int32),
            pltpu.VMEM((1, BL), jnp.int32),
            pltpu.VMEM((2, CH, GRP), f32),
            pltpu.VMEM((2, CH, ANT), f32),
            pltpu.VMEM((2, ANT), f32),
            pltpu.VMEM((4 * NDLY, 4 * CH), bf16),
            pltpu.VMEM((4 * NDLY, N * LANES), bf16),
            pltpu.VMEM((STEPS, ANT_PAD, 2 * TILE), bf16),
            pltpu.VMEM((STEPS, GRP, TILE), bf16),
            pltpu.VMEM((2 * BL, ANT_PAD), bf16),
            pltpu.VMEM((BL, GRP), bf16),
            pltpu.VMEM((6 * CHK, BL), bf16),
            pltpu.VMEM((6 * CHK, 2 * BL), bf16),
            pltpu.VMEM((STEPS, 2 * CHK, 2 * TILE), f32),
            pltpu.VMEM((2, CH, ANT_PAD), f32),
            pltpu.VMEM((4 * CHK, ANT_PAD), bf16),
            pltpu.VMEM((6 * CHK, GRP), f32),
            pltpu.VMEM((2, CH, GRP), f32),
            pltpu.VMEM((4 * CHK, GRP), bf16),
            pltpu.VMEM((6 * CHK, ANT_PAD), f32),
            pltpu.VMEM((CHUNKS, 3, CHK, ANT_PAD), f32),
            pltpu.VMEM((CHUNKS, N, 3, 8, LANES), f32),
            pltpu.VMEM((2 * CH, GRP), f32),
            pltpu.VMEM((GRP, 2 * NDLY), f32),
            pltpu.VMEM((N, OWN, 2 * NDLY), f32),
            pltpu.VMEM((GRP, LANES), f32),
            pltpu.VMEM((OWN, N * LANES), f32),
            pltpu.VMEM((LANES, LANES), f32),
            pltpu.VMEM((8, GRP), f32),
            pltpu.VMEM((GRP, LANES), f32),
            pltpu.VMEM((CH, LANES), f32),
            pltpu.VMEM((N, 8, LANES), f32),
            pltpu.VMEM((N, 8, LANES), f32),
            pltpu.VMEM((N, 16, LANES), f32),
            dma((7 + CHUNKS,)),
            dma((CHUNKS,)), dma((CHUNKS,)), dma((CHUNKS,)), dma((CHUNKS,)),
        ] + [dma((N,))] * 8,
        compiler_params=pltpu.CompilerParams(
            collective_id=0, has_side_effects=True, vmem_limit_bytes=60 * 1024 * 1024),
        cost_estimate=pl.CostEstimate(flops=20_000_000_000, bytes_accessed=4_000_000, transcendentals=0),
    )(vis, ants, gid, sky, start, coords, ahead, back)
    return gains, cal, chi.reshape(CH)


def solution(mesh):
    ahead, back = delay_tables()

    def program(vis, ants, gid, sky, start, coords):
        return jax.shard_map(
            functools.partial(per_device, ahead, back),
            mesh=mesh,
            in_specs=(
                P(None, "chan", "grp"),
                P(None, "grp"),
                P("grp", None),
                P(None, "chan", "grp"),
                P(None, "chan", None),
                P(),
            ),
            out_specs=(P(None, "chan", None), P(None, "chan", "grp"), P("chan")),
            check_vma=False,
        )(vis, ants, gid, sky, start, coords)

    return program
```

```python
import functools

import jax
import jax.numpy as jnp
import numpy as np
from jax import lax
from jax.experimental import pallas as pl
from jax.experimental.pallas import tpu as pltpu
from jax.sharding import PartitionSpec as P

CHANNEL_COUNT = 1536
NDLY = 64
ITERS = 4
RIDGE = 0.5
EPSILON = 1e-06

N = 16
ANT = 350
ANT_PAD = 384
CH = 96
CHUNKS = 3
CHK = CH // CHUNKS
BL = 2048
GRP = 128
TILE = 256
STEPS = BL // TILE
SPAN = 8
OWN = GRP // N
LANES = 128
UNITS = (CHK // 8) * (ANT_PAD // LANES)

GRP_STEPS = sorted(
    ((dx, dy) for dx in range(4) for dy in range(4) if dx or dy),
    key=lambda step: -min(step[0], 4 - step[0]) - min(step[1], 4 - step[1]))
CHAN_STEPS = sorted(
    ((dz, core) for dz in range(8) for core in range(2) if dz or core),
    key=lambda step: -2 * min(step[0], 8 - step[0]) - step[1])

ACROSS = ANT_PAD // LANES

MESH = pl.DeviceIdType.MESH
f32 = jnp.float32
bf16 = jnp.bfloat16


def owner_of(unit):
    return unit + 1 + unit // 4


def two_parts(number):
    first = number.astype(bf16)
    rest = (number - first.astype(f32)).astype(bf16)
    return jnp.concatenate([first, rest], axis=0)


def joined(parts):
    half = parts.shape[0] // 2
    return parts[:half] + parts[half:]


def dot(left, right):
    return jnp.dot(left, right, preferred_element_type=f32)


def dot_last(left, right):
    return lax.dot_general(left, right, (((1,), (1,)), ((), ())), preferred_element_type=f32)


def solve_pair(entry_xx, entry_xy, entry_yy, right_x, right_y):
    ridge_shift = 0.001 * (entry_xx + entry_yy) + EPSILON
    diag_first = entry_xx + ridge_shift
    diag_second = entry_yy + ridge_shift
    determinant = diag_first * diag_second - entry_xy * entry_xy
    return (
        (diag_second * right_x - entry_xy * right_y) / determinant,
        (diag_first * right_y - entry_xy * right_x) / determinant,
    )


def delay_tables():
    channel_ids = np.arange(CHANNEL_COUNT)
    turns = (channel_ids[:, None] * (np.arange(NDLY)[None, :] - NDLY // 2)) % CHANNEL_COUNT
    angles = 2.0 * np.pi / CHANNEL_COUNT * turns
    cosines = np.cos(angles).reshape(N, CH, NDLY).transpose(0, 2, 1)
    sines = np.sin(angles).reshape(N, CH, NDLY).transpose(0, 2, 1)
    ahead = np.concatenate(
        [np.concatenate([cosines, sines], axis=2), np.concatenate([-sines, cosines], axis=2)], axis=1
    )
    back = np.zeros((2 * NDLY, N, LANES))
    back[:NDLY, :, :CH] = sines.transpose(1, 0, 2)
    back[NDLY:, :, :CH] = cosines.transpose(1, 0, 2)
    ahead = ahead / CHANNEL_COUNT
    back = back.reshape(2 * NDLY, N * LANES)
    ahead_1, back_1 = ahead.astype(bf16), back.astype(bf16)
    ahead_2 = (ahead - ahead_1.astype(np.float64)).astype(bf16)
    back_2 = (back - back_1.astype(np.float64)).astype(bf16)
    ahead = np.concatenate(
        [np.concatenate([ahead_1, ahead_1], axis=2), np.concatenate([ahead_2, ahead_2], axis=2)], axis=1)
    return ahead, np.concatenate([back_1, back_2], axis=0)


def kernel(
    vis_hbm, ants_hbm, gid_hbm, sky_hbm, start_hbm, coords_hbm, ahead_hbm, back_hbm,
    gains_out, cal_out, chi_out,
    vis, ants, gid, sky, start, coords, ahead, back,
    hot, grp_hot, hot_t, grp_hot_t, rows_a, rows_b, pair, gain, wide, gain2, acc_grp, unique, unique2, acc_sum, acc_ant, rs_buf,
    ratio, part, coef_buf, model_t, model_band, square, vec_acc, vec_t, chi_acc,
    band_send_buf, band_buf, tot_buf,
    load_sem, rs_send, rs_recv, ag_send, ag_recv, mod_sem, cr_sem, band_sem, tot_sem,
):
    me = lax.axis_index("grp")
    band = lax.axis_index("chan")
    i_own = lax.rem(me, 5) != 0
    my_unit = me - 1 - me // 5

    def others(body):
        for r in range(1, N):
            body(r)

    def grp_other(r):
        dx, dy = GRP_STEPS[r - 1]
        x = me // 4
        return lax.rem(x + dx, 4) * 4 + lax.rem(me - 4 * x + dy, 4)

    def chan_other(r):
        dz, core = CHAN_STEPS[r - 1]
        z = band // 2
        return lax.rem(z + dz, 8) * 2 + lax.rem(band - 2 * z + core, 2)

    loads = [
        pltpu.make_async_copy(ants_hbm, ants, load_sem.at[0]),
        pltpu.make_async_copy(gid_hbm, gid, load_sem.at[1]),
        pltpu.make_async_copy(coords_hbm, coords, load_sem.at[2]),
        pltpu.make_async_copy(start_hbm, start, load_sem.at[3]),
        pltpu.make_async_copy(vis_hbm.at[:, 0:CHK], vis.at[:, 0:CHK], load_sem.at[4]),
        pltpu.make_async_copy(sky_hbm, sky, load_sem.at[5]),
        pltpu.make_async_copy(ahead_hbm.at[band], ahead, load_sem.at[6]),
        pltpu.make_async_copy(back_hbm, back, load_sem.at[7]),
    ] + [
        pltpu.make_async_copy(
            vis_hbm.at[:, c * CHK:(c + 1) * CHK], vis.at[:, c * CHK:(c + 1) * CHK], load_sem.at[7 + c])
        for c in range(1, CHUNKS)
    ]
    for load in loads:
        load.start()

    barrier = pltpu.get_barrier_semaphore()

    def greet(r):
        pl.semaphore_signal(barrier, inc=1, device_id=(grp_other(r), band), device_id_type=MESH)
        pl.semaphore_signal(barrier, inc=1, device_id=(me, chan_other(r)), device_id_type=MESH)

    others(greet)

    vec_acc[...] = jnp.zeros_like(vec_acc)
    wide[:, :, ANT_PAD - LANES:] = jnp.zeros((2, CH, LANES), f32)
    wide[0, :8, :] = jnp.zeros((8, ANT_PAD), f32)
    loads[0].wait()
    loads[1].wait()
    loads[2].wait()
    wide[0, 0:2, :ANT] = coords[...]
    places = two_parts(wide[0, :8, :])

    def build(t, carry):
        cols = pl.ds(pl.multiple_of(t * TILE, TILE), TILE)
        ant_ids = lax.broadcasted_iota(jnp.int32, (ANT_PAD, TILE), 0)
        grp_ids = lax.broadcasted_iota(jnp.int32, (GRP, TILE), 0)
        p_hot = jnp.where(ant_ids == ants[0:1, cols], 1.0, 0.0).astype(bf16)
        q_hot = jnp.where(ant_ids == ants[1:2, cols], 1.0, 0.0).astype(bf16)
        g_hot = jnp.where(grp_ids == gid[0:1, cols], 1.0, 0.0).astype(bf16)
        hot[t, :, :TILE] = p_hot
        hot[t, :, TILE:] = q_hot
        grp_hot[t] = g_hot
        here = pl.multiple_of(2 * t * TILE, TILE)
        hot_t[pl.ds(here, TILE), :] = p_hot.T
        hot_t[pl.ds(here + TILE, TILE), :] = q_hot.T
        grp_hot_t[cols, :] = g_hot.T
        place = joined(dot(places, p_hot - q_hot))
        row = lax.broadcasted_iota(jnp.int32, place.shape, 0)
        place = jnp.where(row == 2, 1.0, place)
        vec_acc[...] += joined(dot_last(two_parts(place), g_hot))
        return carry

    lax.fori_loop(0, STEPS, build, 0, unroll=STEPS)

    loads[3].wait()
    wide[:, :, :ANT] = start[...]
    for chunk in range(CHUNKS):
        for unit in range(UNITS):
            row, lane = chunk * CHK + unit // ACROSS * 8, unit % ACROSS * LANES
            gain[chunk, unit] = wide[:, row:row + 8, lane:lane + LANES]
    loads[4].wait()

    def rows_of(chunk):
        return pl.ds(pl.multiple_of(chunk * CHK, CHK), CHK)

    def group_fit(chunk):
        mine = rows_of(chunk)
        gain2[...] = two_parts(jnp.concatenate(
            [jnp.concatenate([gain[chunk, tile * ACROSS + l, q] for l in range(ACROSS)], axis=1)
             for q in range(2) for tile in range(CHK // 8)], axis=0))

        for t in range(STEPS):
            cols = slice(t * TILE, (t + 1) * TILE)
            pq = joined(dot(gain2[...], hot[t]))
            pair[t] = pq
            a, b = pq[:CHK, :TILE], pq[CHK:, :TILE]
            c, d = pq[:CHK, TILE:], pq[CHK:, TILE:]
            x, y = vis[0, mine, cols], vis[1, mine, cols]
            wr = a * c + b * d
            wi = b * c - a * d
            rows = jnp.concatenate([x * wr + y * wi, y * wr - x * wi, wr * wr + wi * wi], axis=0)
            rows_a[:, cols] = two_parts(rows)
            if (t + 1) % SPAN == 0:
                part_cols = slice((t + 1 - SPAN) * TILE, (t + 1) * TILE)
                acc_grp[...] = dot(rows_a[:, part_cols], grp_hot_t[part_cols, :])

        sums = joined(acc_grp[...])
        scale = 1.0 / (sums[2 * CHK:] + RIDGE)
        ur, ui = sums[:CHK] * scale, sums[CHK:2 * CHK] * scale
        unique[0, mine, :] = ur
        unique[1, mine, :] = ui
        unique2[...] = two_parts(jnp.concatenate([ur, ui], axis=0))

    def antenna_sums(chunk):
        mine = rows_of(chunk)

        for t in range(STEPS):
            cols = slice(t * TILE, (t + 1) * TILE)
            uu = joined(dot(unique2[...], grp_hot[t]))
            s, v = uu[:CHK], uu[CHK:]
            pq = pair[t]
            a, b = pq[:CHK, :TILE], pq[CHK:, :TILE]
            c, d = pq[:CHK, TILE:], pq[CHK:, TILE:]
            x, y = vis[0, mine, cols], vis[1, mine, cols]
            zr = s * x + v * y
            zi = s * y - v * x
            size = s * s + v * v
            for_p = jnp.concatenate([c * zr - d * zi, c * zi + d * zr, size * (c * c + d * d)], axis=0)
            for_q = jnp.concatenate([a * zr + b * zi, b * zr - a * zi, size * (a * a + b * b)], axis=0)
            rows_b[:, 2 * t * TILE:(2 * t + 1) * TILE] = two_parts(for_p)
            rows_b[:, (2 * t + 1) * TILE:(2 * t + 2) * TILE] = two_parts(for_q)
            if (t + 1) % SPAN == 0:
                part_cols = slice(2 * (t + 1 - SPAN) * TILE, 2 * (t + 1) * TILE)
                acc_sum[...] = dot(rows_b[:, part_cols], hot_t[part_cols, :])

        sums = joined(acc_sum[...]).reshape(3, CHK, ANT_PAD)
        for unit in range(UNITS):
            row, lane = unit // ACROSS * 8, unit % ACROSS * LANES
            acc_ant[chunk, unit] = sums[:, row:row + 8, lane:lane + LANES]

    def misfit(chunk):
        mine = rows_of(chunk)
        chi_acc[mine, :] = jnp.zeros((CHK, LANES), f32)

        def step(t, carry):
            cols = pl.ds(pl.multiple_of(t * TILE, TILE), TILE)
            uu = joined(dot(unique2[...], grp_hot[t]))
            s, v = uu[:CHK], uu[CHK:]
            pq = pair[t]
            a, b = pq[:CHK, :TILE], pq[CHK:, :TILE]
            c, d = pq[:CHK, TILE:], pq[CHK:, TILE:]
            wr = a * c + b * d
            wi = b * c - a * d
            er = vis[0, mine, cols] - (wr * s - wi * v)
            ei = vis[1, mine, cols] - (wr * v + wi * s)
            e = er * er + ei * ei
            chi_acc[mine, :] += e[:, :LANES] + e[:, LANES:]
            return carry

        lax.fori_loop(0, STEPS, step, 0, unroll=STEPS)

    def rs_copy(chunk, unit):
        return pltpu.make_async_remote_copy(
            src_ref=acc_ant.at[chunk, unit],
            dst_ref=rs_buf.at[chunk, me],
            send_sem=rs_send.at[chunk], recv_sem=rs_recv.at[chunk],
            device_id=(owner_of(unit), band), device_id_type=MESH)

    def arrivals(sem, shape):
        return pltpu.make_async_copy(shape, shape, sem)

    def ag_copy(chunk, unit, other):
        return pltpu.make_async_remote_copy(
            src_ref=gain.at[chunk, unit], dst_ref=gain.at[chunk, unit],
            send_sem=ag_send.at[chunk], recv_sem=ag_recv.at[chunk],
            device_id=(other, band), device_id_type=MESH)

    def units(body):
        def one(r):
            other = grp_other(r)

            @pl.when(lax.rem(other, 5) != 0)
            def _():
                body(other - 1 - other // 5)

        others(one)

    def send_sums(chunk):
        units(lambda unit: rs_copy(chunk, unit).start())

    def update_gains(chunk):
        @pl.when(i_own)
        def _():
            rs_buf[chunk, me] = acc_ant[chunk, my_unit]
            arrivals(rs_recv.at[chunk], rs_buf.at[chunk, 0:N - 1]).wait()
            total = rs_buf[chunk, 0]
            for source in range(1, N):
                total = total + rs_buf[chunk, source]
            share = 0.5 / (total[2] + RIDGE)
            gain[chunk, my_unit] = 0.5 * gain[chunk, my_unit] + total[:2] * share
            others(lambda r: ag_copy(chunk, my_unit, grp_other(r)).start())

    def by_place(body):
        @pl.when(i_own)
        def _():
            body(UNITS - 1)

        @pl.when(jnp.logical_not(i_own))
        def _():
            body(UNITS)

    def await_gains(chunk):
        by_place(lambda n: arrivals(ag_recv.at[chunk], rs_buf.at[chunk, 0:n, 0:2]).wait())

    def settle(chunk):
        by_place(lambda n: arrivals(rs_send.at[chunk], rs_buf.at[chunk, 0:n]).wait())

        @pl.when(i_own)
        def _():
            arrivals(ag_send.at[chunk], rs_buf.at[chunk, 0:N - 1, 0:2]).wait()

    def mod_copy(source, other):
        return pltpu.make_async_remote_copy(
            src_ref=model_t.at[pl.ds(pl.multiple_of(other * OWN, OWN), OWN), :],
            dst_ref=model_band.at[:, pl.ds(pl.multiple_of(source * LANES, LANES), LANES)],
            send_sem=mod_sem.at[0], recv_sem=mod_sem.at[1],
            device_id=(me, other), device_id_type=MESH)

    def iteration(s, carry):
        chunk = lax.rem(s, CHUNKS)

        @pl.when(s >= CHUNKS)
        def _():
            await_gains(chunk)

        for c in range(1, CHUNKS):
            @pl.when(s == c)
            def _():
                loads[7 + c].wait()

        group_fit(chunk)

        @pl.when(s >= CHUNKS)
        def _():
            settle(chunk)

        antenna_sums(chunk)

        @pl.when(s == 0)
        def _():
            pl.semaphore_wait(barrier, 2 * (N - 1))

        send_sums(chunk)

        @pl.when(s == CHUNKS - 1)
        def _():
            loads[5].wait()
            model = sky[0] * sky[0] + sky[1] * sky[1]
            square[CH:, :] = jnp.zeros((LANES - CH, LANES), f32)
            square[:CH, :] = model
            model_t[...] = square[...].T
            own_rows = pl.ds(pl.multiple_of(band * OWN, OWN), OWN)
            own_lanes = pl.ds(pl.multiple_of(band * LANES, LANES), LANES)
            model_band[:, own_lanes] = model_t[own_rows, :]
            others(lambda r: mod_copy(band, chan_other(r)).start())

        final = ITERS * CHUNKS - 1

        @pl.when(jnp.logical_and(s >= 1, s <= final - CHUNKS + 1))
        def _():
            update_gains(lax.rem(s + CHUNKS - 1, CHUNKS))

        @pl.when(s == final)
        def _():
            def each(c, carry):
                update_gains(c)
                return carry

            lax.fori_loop(0, CHUNKS, each, 0)

        return carry

    lax.fori_loop(0, ITERS * CHUNKS, iteration, 0)

    def last(chunk, carry):
        await_gains(chunk)
        group_fit(chunk)

        settle(chunk)

        @pl.when(chunk < CHUNKS - 1)
        def _():
            misfit(chunk)

        return carry

    lax.fori_loop(0, CHUNKS, last, 0)

    ur, ui = unique[0], unique[1]
    sr, si = sky[0], sky[1]
    ratio[:CH, :] = ur * sr + ui * si
    ratio[CH:, :] = ui * sr - ur * si
    loads[6].wait()
    part[...] = joined(dot(ahead[...], two_parts(ratio[...]))).T

    def cr_copy(source, other):
        return pltpu.make_async_remote_copy(
            src_ref=part.at[pl.ds(pl.multiple_of(other * OWN, OWN), OWN), :], dst_ref=coef_buf.at[source],
            send_sem=cr_sem.at[0], recv_sem=cr_sem.at[1],
            device_id=(me, other), device_id_type=MESH)

    others(lambda r: cr_copy(band, chan_other(r)).start())
    coef_buf[band] = part[pl.ds(pl.multiple_of(band * OWN, OWN), OWN), :]
    misfit(CHUNKS - 1)

    for chunk in range(CHUNKS):
        for unit in range(UNITS):
            row, lane = chunk * CHK + unit // ACROSS * 8, unit % ACROSS * LANES
            wide[:, row:row + 8, lane:lane + LANES] = gain[chunk, unit]
    gains_out[...] = wide[:, :, :ANT]
    east = vec_acc[0:1, :] / vec_acc[2:3, :]
    north = vec_acc[1:2, :] / vec_acc[2:3, :]
    square[...] = jnp.zeros_like(square)
    square[0:1, :] = east
    square[1:2, :] = north
    vec_t[...] = square[...].T
    model = sr * sr + si * si
    squared = model * model
    fields = [
        ur * ur + ui * ui, model, squared * (east * east), squared * (east * north),
        squared * (north * north), chi_acc[...],
    ]
    lane = lax.broadcasted_iota(jnp.int32, (CH, LANES), 1)
    table = jnp.zeros((CH, LANES), f32)
    for place, field in enumerate(fields):
        table = jnp.where(lane == place, jnp.sum(field, axis=1, keepdims=True), table)
    square[CH:, :] = jnp.zeros((LANES - CH, LANES), f32)
    square[:CH, :] = table
    local = square[...].T[:8, :]

    channel = band * CH + lax.broadcasted_iota(jnp.int32, (1, LANES), 1)
    frequency = 1.0 + channel.astype(f32) * (1.0 / CHANNEL_COUNT)
    squares = frequency * frequency
    slope_parts = squares * local[2:5]
    at = lax.broadcasted_iota(jnp.int32, (1, N * LANES), 1)
    band_channel = (at // LANES) * CH + lax.rem(at, LANES)
    band_frequency = 1.0 + band_channel.astype(f32) * (1.0 / CHANNEL_COUNT)
    my_groups = vec_t[pl.ds(pl.multiple_of(band * OWN, OWN), OWN), :]

    loads[7].wait()
    arrivals(mod_sem.at[1], coef_buf.at[0:N - 1]).wait()
    arrivals(mod_sem.at[0], coef_buf.at[0:N - 1]).wait()
    weights_east = model_band[...] * my_groups[:, 0:1]
    weights_north = model_band[...] * my_groups[:, 1:2]

    arrivals(cr_sem.at[1], coef_buf.at[0:N - 1]).wait()
    coef = coef_buf[0]
    for source in range(1, N):
        coef = coef + coef_buf[source]
    coef = two_parts(coef)
    phases = joined(dot(jnp.concatenate([coef, coef], axis=1), back[...]))
    right_east = jnp.sum(weights_east * phases, axis=0, keepdims=True)
    right_north = jnp.sum(weights_north * phases, axis=0, keepdims=True)
    slope_east = jnp.sum(band_frequency * right_east, axis=1, keepdims=True)
    slope_north = jnp.sum(band_frequency * right_north, axis=1, keepdims=True)
    first_lane = lax.broadcasted_iota(jnp.int32, (1, LANES), 1) == 0
    slope_rows = jnp.concatenate(
        [jnp.where(first_lane, slope_east, 0.0), jnp.where(first_lane, slope_north, 0.0),
         slope_parts, jnp.zeros((1, LANES), f32)], axis=0)
    for other in range(N):
        lanes = slice(other * LANES, (other + 1) * LANES)
        band_send_buf[other] = jnp.concatenate([right_east[:, lanes], right_north[:, lanes], slope_rows], axis=0)

    def band_copy(source, other):
        return pltpu.make_async_remote_copy(
            src_ref=band_send_buf.at[other], dst_ref=band_buf.at[source],
            send_sem=band_sem.at[0], recv_sem=band_sem.at[1],
            device_id=(me, other), device_id_type=MESH)

    others(lambda r: band_copy(band, chan_other(r)).start())
    band_buf[band] = band_send_buf[band]
    arrivals(cr_sem.at[0], coef_buf.at[0:N - 1]).wait()
    arrivals(band_sem.at[1], coef_buf.at[0:N - 1]).wait()
    sums = band_buf[0]
    for source in range(1, N):
        sums = sums + band_buf[source]

    tot_buf[me] = jnp.concatenate(
        [local[0:5], sums[0:2], local[5:6], sums[2:7], jnp.zeros((3, LANES), f32)], axis=0)

    def tot_copy(source, other):
        return pltpu.make_async_remote_copy(
            src_ref=tot_buf.at[source], dst_ref=tot_buf.at[source],
            send_sem=tot_sem.at[0], recv_sem=tot_sem.at[1],
            device_id=(other, band), device_id_type=MESH)

    others(lambda r: tot_copy(me, grp_other(r)).start())
    arrivals(band_sem.at[0], coef_buf.at[0:N - 1]).wait()
    arrivals(tot_sem.at[1], tot_buf.at[0:N - 1]).wait()
    totals = tot_buf[0]
    for source in range(1, N):
        totals = totals + tot_buf[source]
    arrivals(tot_sem.at[0], tot_buf.at[0:N - 1]).wait()
    chi_out[...] = totals[7:8, :CH]

    terms = jnp.sum(totals[8:16], axis=1, keepdims=True)
    slope_east, slope_north = solve_pair(
        terms[2:3], terms[3:4], terms[4:5], terms[0:1], terms[1:2])
    tilt_east, tilt_north = solve_pair(
        totals[2:3], totals[3:4], totals[4:5], totals[5:6], totals[6:7])
    tilt_east = tilt_east - frequency * slope_east
    tilt_north = tilt_north - frequency * slope_north
    amplitude = jnp.sqrt((totals[0:1] + EPSILON) / (totals[1:2] + EPSILON))
    square[0:8, :] = jnp.concatenate(
        [frequency, tilt_east, tilt_north, 1.0 / amplitude, jnp.zeros((4, LANES), f32)], axis=0)
    columns = square[...].T[:CH, :]
    along = slope_east * east + slope_north * north
    turn = columns[:, 0:1] * along + columns[:, 1:2] * east + columns[:, 2:3] * north
    rotation_cos = jnp.cos(turn) * columns[:, 3:4]
    rotation_sin = jnp.sin(turn) * columns[:, 3:4]
    cal_out[0] = ur * rotation_cos + ui * rotation_sin
    cal_out[1] = ui * rotation_cos - ur * rotation_sin


def per_device(ahead, back, vis, ants, gid, sky, start, coords):
    vmem = pl.BlockSpec(memory_space=pltpu.VMEM)
    hbm = pl.BlockSpec(memory_space=pltpu.HBM)
    dma = pltpu.SemaphoreType.DMA
    gains, cal, chi = pl.pallas_call(
        kernel,
        out_shape=(
            jax.ShapeDtypeStruct((2, CH, ANT), f32),
            jax.ShapeDtypeStruct((2, CH, GRP), f32),
            jax.ShapeDtypeStruct((1, CH), f32),
        ),
        in_specs=[hbm] * 8,
        out_specs=(vmem, vmem, vmem),
        scratch_shapes=[
            pltpu.VMEM((2, CH, BL), f32),
            pltpu.VMEM((2, BL), jnp.int32),
            pltpu.VMEM((1, BL), jnp.int32),
            pltpu.VMEM((2, CH, GRP), f32),
            pltpu.VMEM((2, CH, ANT), f32),
            pltpu.VMEM((2, ANT), f32),
            pltpu.VMEM((4 * NDLY, 4 * CH), bf16),
            pltpu.VMEM((4 * NDLY, N * LANES), bf16),
            pltpu.VMEM((STEPS, ANT_PAD, 2 * TILE), bf16),
            pltpu.VMEM((STEPS, GRP, TILE), bf16),
            pltpu.VMEM((2 * BL, ANT_PAD), bf16),
            pltpu.VMEM((BL, GRP), bf16),
            pltpu.VMEM((6 * CHK, BL), bf16),
            pltpu.VMEM((6 * CHK, 2 * BL), bf16),
            pltpu.VMEM((STEPS, 2 * CHK, 2 * TILE), f32),
            pltpu.VMEM((CHUNKS, UNITS, 2, 8, LANES), f32),
            pltpu.VMEM((2, CH, ANT_PAD), f32),
            pltpu.VMEM((4 * CHK, ANT_PAD), bf16),
            pltpu.VMEM((6 * CHK, GRP), f32),
            pltpu.VMEM((2, CH, GRP), f32),
            pltpu.VMEM((4 * CHK, GRP), bf16),
            pltpu.VMEM((6 * CHK, ANT_PAD), f32),
            pltpu.VMEM((CHUNKS, UNITS, 3, 8, LANES), f32),
            pltpu.VMEM((CHUNKS, N, 3, 8, LANES), f32),
            pltpu.VMEM((2 * CH, GRP), f32),
            pltpu.VMEM((GRP, 2 * NDLY), f32),
            pltpu.VMEM((N, OWN, 2 * NDLY), f32),
            pltpu.VMEM((GRP, LANES), f32),
            pltpu.VMEM((OWN, N * LANES), f32),
            pltpu.VMEM((LANES, LANES), f32),
            pltpu.VMEM((8, GRP), f32),
            pltpu.VMEM((GRP, LANES), f32),
            pltpu.VMEM((CH, LANES), f32),
            pltpu.VMEM((N, 8, LANES), f32),
            pltpu.VMEM((N, 8, LANES), f32),
            pltpu.VMEM((N, 16, LANES), f32),
            dma((7 + CHUNKS,)),
            dma((CHUNKS,)), dma((CHUNKS,)), dma((CHUNKS,)), dma((CHUNKS,)),
        ] + [dma((2,))] * 4,
        compiler_params=pltpu.CompilerParams(
            collective_id=0, has_side_effects=True, vmem_limit_bytes=60 * 1024 * 1024),
        cost_estimate=pl.CostEstimate(flops=20_000_000_000, bytes_accessed=4_000_000, transcendentals=0),
    )(vis, ants, gid, sky, start, coords, ahead, back)
    return gains, cal, chi.reshape(CH)


def solution(mesh):
    ahead, back = delay_tables()

    def program(vis, ants, gid, sky, start, coords):
        return jax.shard_map(
            functools.partial(per_device, ahead, back),
            mesh=mesh,
            in_specs=(
                P(None, "chan", "grp"),
                P(None, "grp"),
                P("grp", None),
                P(None, "chan", "grp"),
                P(None, "chan", None),
                P(),
            ),
            out_specs=(P(None, "chan", None), P(None, "chan", "grp"), P("chan")),
            check_vma=False,
        )(vis, ants, gid, sky, start, coords)

    return program
```

```python
import functools

import jax
import jax.numpy as jnp
import numpy as np
from jax import lax
from jax.experimental import pallas as pl
from jax.experimental.pallas import tpu as pltpu
from jax.sharding import PartitionSpec as P

CHANNEL_COUNT = 1536
NDLY = 64
ITERS = 4
RIDGE = 0.5
EPSILON = 1e-06

N = 16
ANT = 350
ANT_PAD = 384
CH = 96
CHUNKS = 3
CHK = CH // CHUNKS
BL = 2048
GRP = 128
TILE = 256
STEPS = BL // TILE
SPAN = 8
OWN = GRP // N
LANES = 128
UNITS = (CHK // 8) * (ANT_PAD // LANES)

GRP_STEPS = sorted(
    ((dx, dy) for dx in range(4) for dy in range(4) if dx or dy),
    key=lambda step: -min(step[0], 4 - step[0]) - min(step[1], 4 - step[1]))
CHAN_STEPS = sorted(
    ((dz, core) for dz in range(8) for core in range(2) if dz or core),
    key=lambda step: -2 * min(step[0], 8 - step[0]) - step[1])

ACROSS = ANT_PAD // LANES

MESH = pl.DeviceIdType.MESH
f32 = jnp.float32
bf16 = jnp.bfloat16


def owner_of(unit):
    return unit + 1 + unit // 4


def two_parts(number):
    first = number.astype(bf16)
    rest = (number - first.astype(f32)).astype(bf16)
    return jnp.concatenate([first, rest], axis=0)


def joined(parts):
    half = parts.shape[0] // 2
    return parts[:half] + parts[half:]


def dot(left, right):
    return jnp.dot(left, right, preferred_element_type=f32)


def dot_last(left, right):
    return lax.dot_general(left, right, (((1,), (1,)), ((), ())), preferred_element_type=f32)


def solve_pair(entry_xx, entry_xy, entry_yy, right_x, right_y):
    ridge_shift = 0.001 * (entry_xx + entry_yy) + EPSILON
    diag_first = entry_xx + ridge_shift
    diag_second = entry_yy + ridge_shift
    determinant = diag_first * diag_second - entry_xy * entry_xy
    return (
        (diag_second * right_x - entry_xy * right_y) / determinant,
        (diag_first * right_y - entry_xy * right_x) / determinant,
    )


def delay_tables():
    channel_ids = np.arange(CHANNEL_COUNT)
    turns = (channel_ids[:, None] * (np.arange(NDLY)[None, :] - NDLY // 2)) % CHANNEL_COUNT
    angles = 2.0 * np.pi / CHANNEL_COUNT * turns
    cosines = np.cos(angles).reshape(N, CH, NDLY).transpose(0, 2, 1)
    sines = np.sin(angles).reshape(N, CH, NDLY).transpose(0, 2, 1)
    ahead = np.concatenate(
        [np.concatenate([cosines, sines], axis=2), np.concatenate([-sines, cosines], axis=2)], axis=1
    )
    back = np.zeros((2 * NDLY, N, LANES))
    back[:NDLY, :, :CH] = sines.transpose(1, 0, 2)
    back[NDLY:, :, :CH] = cosines.transpose(1, 0, 2)
    ahead = ahead / CHANNEL_COUNT
    back = back.reshape(2 * NDLY, N * LANES)
    ahead_1, back_1 = ahead.astype(bf16), back.astype(bf16)
    ahead_2 = (ahead - ahead_1.astype(np.float64)).astype(bf16)
    back_2 = (back - back_1.astype(np.float64)).astype(bf16)
    ahead = np.concatenate(
        [np.concatenate([ahead_1, ahead_1], axis=2), np.concatenate([ahead_2, ahead_2], axis=2)], axis=1)
    return ahead, np.concatenate([back_1, back_2], axis=0)


def kernel(
    vis_hbm, ants_hbm, gid_hbm, sky_hbm, start_hbm, coords_hbm, ahead_hbm, back_hbm,
    gains_out, cal_out, chi_out,
    vis, ants, gid, sky, start, coords, ahead, back,
    hot, grp_hot, hot_t, grp_hot_t, rows_a, rows_b, pair, gain, wide, gain2, acc_grp, unique, unique2, acc_sum, acc_ant, rs_buf,
    ratio, part, coef_buf, model_t, model_band, square, vec_acc, vec_t, chi_acc,
    band_send_buf, band_buf, tot_buf,
    load_sem, rs_send, rs_recv, ag_send, ag_recv, mod_sem, cr_sem, band_sem, tot_sem,
):
    me = lax.axis_index("grp")
    band = lax.axis_index("chan")
    i_own = lax.rem(me, 5) != 0
    my_unit = me - 1 - me // 5

    def others(body):
        for r in range(1, N):
            body(r)

    def grp_other(r):
        dx, dy = GRP_STEPS[r - 1]
        x = me // 4
        return lax.rem(x + dx, 4) * 4 + lax.rem(me - 4 * x + dy, 4)

    def chan_other(r):
        dz, core = CHAN_STEPS[r - 1]
        z = band // 2
        return lax.rem(z + dz, 8) * 2 + lax.rem(band - 2 * z + core, 2)

    loads = [
        pltpu.make_async_copy(ants_hbm, ants, load_sem.at[0]),
        pltpu.make_async_copy(gid_hbm, gid, load_sem.at[1]),
        pltpu.make_async_copy(coords_hbm, coords, load_sem.at[2]),
        pltpu.make_async_copy(start_hbm, start, load_sem.at[3]),
        pltpu.make_async_copy(vis_hbm.at[:, 0:CHK], vis.at[:, 0:CHK], load_sem.at[4]),
        pltpu.make_async_copy(sky_hbm, sky, load_sem.at[5]),
        pltpu.make_async_copy(ahead_hbm.at[band], ahead, load_sem.at[6]),
        pltpu.make_async_copy(back_hbm, back, load_sem.at[7]),
    ] + [
        pltpu.make_async_copy(
            vis_hbm.at[:, c * CHK:(c + 1) * CHK], vis.at[:, c * CHK:(c + 1) * CHK], load_sem.at[7 + c])
        for c in range(1, CHUNKS)
    ]
    for load in loads:
        load.start()

    barrier = pltpu.get_barrier_semaphore()

    def greet(r):
        pl.semaphore_signal(barrier, inc=1, device_id=(grp_other(r), band), device_id_type=MESH)
        pl.semaphore_signal(barrier, inc=1, device_id=(me, chan_other(r)), device_id_type=MESH)

    others(greet)

    vec_acc[...] = jnp.zeros_like(vec_acc)
    wide[:, :, ANT_PAD - LANES:] = jnp.zeros((2, CH, LANES), f32)
    wide[0, :8, :] = jnp.zeros((8, ANT_PAD), f32)
    loads[0].wait()
    loads[1].wait()
    loads[2].wait()
    wide[0, 0:2, :ANT] = coords[...]
    places = two_parts(wide[0, :8, :])

    def build(t, carry):
        cols = pl.ds(pl.multiple_of(t * TILE, TILE), TILE)
        ant_ids = lax.broadcasted_iota(jnp.int32, (ANT_PAD, TILE), 0)
        grp_ids = lax.broadcasted_iota(jnp.int32, (GRP, TILE), 0)
        p_hot = jnp.where(ant_ids == ants[0:1, cols], 1.0, 0.0).astype(bf16)
        q_hot = jnp.where(ant_ids == ants[1:2, cols], 1.0, 0.0).astype(bf16)
        g_hot = jnp.where(grp_ids == gid[0:1, cols], 1.0, 0.0).astype(bf16)
        hot[t, :, :TILE] = p_hot
        hot[t, :, TILE:] = q_hot
        grp_hot[t] = g_hot
        here = pl.multiple_of(2 * t * TILE, TILE)
        hot_t[pl.ds(here, TILE), :] = p_hot.T
        hot_t[pl.ds(here + TILE, TILE), :] = q_hot.T
        grp_hot_t[cols, :] = g_hot.T
        place = joined(dot(places, p_hot - q_hot))
        row = lax.broadcasted_iota(jnp.int32, place.shape, 0)
        place = jnp.where(row == 2, 1.0, place)
        vec_acc[...] += joined(dot_last(two_parts(place), g_hot))
        return carry

    lax.fori_loop(0, STEPS, build, 0, unroll=STEPS)

    loads[3].wait()
    wide[:, :, :ANT] = start[...]
    for chunk in range(CHUNKS):
        for unit in range(UNITS):
            row, lane = chunk * CHK + unit // ACROSS * 8, unit % ACROSS * LANES
            gain[chunk, unit] = wide[:, row:row + 8, lane:lane + LANES]
    loads[4].wait()

    def rows_of(chunk):
        return pl.ds(pl.multiple_of(chunk * CHK, CHK), CHK)

    def group_fit(chunk):
        mine = rows_of(chunk)
        gain2[...] = two_parts(jnp.concatenate(
            [jnp.concatenate([gain[chunk, tile * ACROSS + l, q] for l in range(ACROSS)], axis=1)
             for q in range(2) for tile in range(CHK // 8)], axis=0))

        for t in range(STEPS):
            cols = slice(t * TILE, (t + 1) * TILE)
            pq = joined(dot(gain2[...], hot[t]))
            pair[t] = pq
            a, b = pq[:CHK, :TILE], pq[CHK:, :TILE]
            c, d = pq[:CHK, TILE:], pq[CHK:, TILE:]
            x, y = vis[0, mine, cols], vis[1, mine, cols]
            wr = a * c + b * d
            wi = b * c - a * d
            rows = jnp.concatenate([x * wr + y * wi, y * wr - x * wi, wr * wr + wi * wi], axis=0)
            rows_a[:, cols] = two_parts(rows)
            if (t + 1) % SPAN == 0:
                part_cols = slice((t + 1 - SPAN) * TILE, (t + 1) * TILE)
                acc_grp[...] = dot(rows_a[:, part_cols], grp_hot_t[part_cols, :])

        sums = joined(acc_grp[...])
        scale = 1.0 / (sums[2 * CHK:] + RIDGE)
        ur, ui = sums[:CHK] * scale, sums[CHK:2 * CHK] * scale
        unique[0, mine, :] = ur
        unique[1, mine, :] = ui
        unique2[...] = two_parts(jnp.concatenate([ur, ui], axis=0))

    def antenna_sums(chunk):
        mine = rows_of(chunk)

        for t in range(STEPS):
            cols = slice(t * TILE, (t + 1) * TILE)
            uu = joined(dot(unique2[...], grp_hot[t]))
            s, v = uu[:CHK], uu[CHK:]
            pq = pair[t]
            a, b = pq[:CHK, :TILE], pq[CHK:, :TILE]
            c, d = pq[:CHK, TILE:], pq[CHK:, TILE:]
            x, y = vis[0, mine, cols], vis[1, mine, cols]
            zr = s * x + v * y
            zi = s * y - v * x
            size = s * s + v * v
            for_p = jnp.concatenate([c * zr - d * zi, c * zi + d * zr, size * (c * c + d * d)], axis=0)
            for_q = jnp.concatenate([a * zr + b * zi, b * zr - a * zi, size * (a * a + b * b)], axis=0)
            rows_b[:, 2 * t * TILE:(2 * t + 1) * TILE] = two_parts(for_p)
            rows_b[:, (2 * t + 1) * TILE:(2 * t + 2) * TILE] = two_parts(for_q)
            if (t + 1) % SPAN == 0:
                part_cols = slice(2 * (t + 1 - SPAN) * TILE, 2 * (t + 1) * TILE)
                acc_sum[...] = dot(rows_b[:, part_cols], hot_t[part_cols, :])

        sums = joined(acc_sum[...]).reshape(3, CHK, ANT_PAD)
        for unit in range(UNITS):
            row, lane = unit // ACROSS * 8, unit % ACROSS * LANES
            acc_ant[chunk, unit] = sums[:, row:row + 8, lane:lane + LANES]

    def misfit(chunk):
        mine = rows_of(chunk)
        chi_acc[mine, :] = jnp.zeros((CHK, LANES), f32)

        def step(t, carry):
            cols = pl.ds(pl.multiple_of(t * TILE, TILE), TILE)
            uu = joined(dot(unique2[...], grp_hot[t]))
            s, v = uu[:CHK], uu[CHK:]
            pq = pair[t]
            a, b = pq[:CHK, :TILE], pq[CHK:, :TILE]
            c, d = pq[:CHK, TILE:], pq[CHK:, TILE:]
            wr = a * c + b * d
            wi = b * c - a * d
            er = vis[0, mine, cols] - (wr * s - wi * v)
            ei = vis[1, mine, cols] - (wr * v + wi * s)
            e = er * er + ei * ei
            chi_acc[mine, :] += e[:, :LANES] + e[:, LANES:]
            return carry

        lax.fori_loop(0, STEPS, step, 0, unroll=STEPS)

    def rs_copy(chunk, unit):
        return pltpu.make_async_remote_copy(
            src_ref=acc_ant.at[chunk, unit],
            dst_ref=rs_buf.at[chunk, me],
            send_sem=rs_send.at[chunk], recv_sem=rs_recv.at[chunk],
            device_id=(owner_of(unit), band), device_id_type=MESH)

    def arrivals(sem, shape):
        return pltpu.make_async_copy(shape, shape, sem)

    def ag_copy(chunk, unit, other):
        return pltpu.make_async_remote_copy(
            src_ref=gain.at[chunk, unit], dst_ref=gain.at[chunk, unit],
            send_sem=ag_send.at[chunk], recv_sem=ag_recv.at[chunk],
            device_id=(other, band), device_id_type=MESH)

    def units(body):
        def one(r):
            other = grp_other(r)

            @pl.when(lax.rem(other, 5) != 0)
            def _():
                body(other - 1 - other // 5)

        others(one)

    def send_sums(chunk):
        units(lambda unit: rs_copy(chunk, unit).start())

    def update_gains(chunk):
        @pl.when(i_own)
        def _():
            rs_buf[chunk, me] = acc_ant[chunk, my_unit]
            arrivals(rs_recv.at[chunk], rs_buf.at[chunk, 0:N - 1]).wait()
            total = rs_buf[chunk, 0]
            for source in range(1, N):
                total = total + rs_buf[chunk, source]
            share = 0.5 / (total[2] + RIDGE)
            gain[chunk, my_unit] = 0.5 * gain[chunk, my_unit] + total[:2] * share
            others(lambda r: ag_copy(chunk, my_unit, grp_other(r)).start())

    def by_place(body):
        @pl.when(i_own)
        def _():
            body(UNITS - 1)

        @pl.when(jnp.logical_not(i_own))
        def _():
            body(UNITS)

    def await_gains(chunk):
        by_place(lambda n: arrivals(ag_recv.at[chunk], rs_buf.at[chunk, 0:n, 0:2]).wait())

    def settle(chunk):
        by_place(lambda n: arrivals(rs_send.at[chunk], rs_buf.at[chunk, 0:n]).wait())

        @pl.when(i_own)
        def _():
            arrivals(ag_send.at[chunk], rs_buf.at[chunk, 0:N - 1, 0:2]).wait()

    def mod_copy(source, other):
        return pltpu.make_async_remote_copy(
            src_ref=model_t.at[pl.ds(pl.multiple_of(other * OWN, OWN), OWN), :],
            dst_ref=model_band.at[:, pl.ds(pl.multiple_of(source * LANES, LANES), LANES)],
            send_sem=mod_sem.at[0], recv_sem=mod_sem.at[1],
            device_id=(me, other), device_id_type=MESH)

    def iteration(s, carry):
        chunk = lax.rem(s, CHUNKS)

        @pl.when(s >= CHUNKS)
        def _():
            await_gains(chunk)

        for c in range(1, CHUNKS):
            @pl.when(s == c)
            def _():
                loads[7 + c].wait()

        group_fit(chunk)

        @pl.when(s >= CHUNKS)
        def _():
            settle(chunk)

        antenna_sums(chunk)

        @pl.when(s == 0)
        def _():
            pl.semaphore_wait(barrier, 2 * (N - 1))

        send_sums(chunk)

        @pl.when(s == CHUNKS - 1)
        def _():
            loads[5].wait()
            model = sky[0] * sky[0] + sky[1] * sky[1]
            square[CH:, :] = jnp.zeros((LANES - CH, LANES), f32)
            square[:CH, :] = model
            model_t[...] = square[...].T
            own_rows = pl.ds(pl.multiple_of(band * OWN, OWN), OWN)
            own_lanes = pl.ds(pl.multiple_of(band * LANES, LANES), LANES)
            model_band[:, own_lanes] = model_t[own_rows, :]
            others(lambda r: mod_copy(band, chan_other(r)).start())

        final = ITERS * CHUNKS - 1

        @pl.when(jnp.logical_and(s >= 1, s <= final - CHUNKS + 1))
        def _():
            update_gains(lax.rem(s + CHUNKS - 1, CHUNKS))

        @pl.when(s == final)
        def _():
            def each(c, carry):
                update_gains(c)
                return carry

            lax.fori_loop(0, CHUNKS, each, 0)

        return carry

    lax.fori_loop(0, ITERS * CHUNKS, iteration, 0)

    def last(chunk, carry):
        await_gains(chunk)
        group_fit(chunk)

        settle(chunk)

        @pl.when(chunk < CHUNKS - 1)
        def _():
            misfit(chunk)

        return carry

    lax.fori_loop(0, CHUNKS, last, 0)

    ur, ui = unique[0], unique[1]
    sr, si = sky[0], sky[1]
    ratio[:CH, :] = ur * sr + ui * si
    ratio[CH:, :] = ui * sr - ur * si
    loads[6].wait()
    part[...] = joined(dot(ahead[...], two_parts(ratio[...]))).T

    def cr_copy(source, other):
        return pltpu.make_async_remote_copy(
            src_ref=part.at[pl.ds(pl.multiple_of(other * OWN, OWN), OWN), :], dst_ref=coef_buf.at[source],
            send_sem=cr_sem.at[0], recv_sem=cr_sem.at[1],
            device_id=(me, other), device_id_type=MESH)

    others(lambda r: cr_copy(band, chan_other(r)).start())
    coef_buf[band] = part[pl.ds(pl.multiple_of(band * OWN, OWN), OWN), :]
    misfit(CHUNKS - 1)

    for chunk in range(CHUNKS):
        for unit in range(UNITS):
            row, lane = chunk * CHK + unit // ACROSS * 8, unit % ACROSS * LANES
            wide[:, row:row + 8, lane:lane + LANES] = gain[chunk, unit]
    gains_out[...] = wide[:, :, :ANT]
    east = vec_acc[0:1, :] / vec_acc[2:3, :]
    north = vec_acc[1:2, :] / vec_acc[2:3, :]
    square[...] = jnp.zeros_like(square)
    square[0:1, :] = east
    square[1:2, :] = north
    vec_t[...] = square[...].T
    model = sr * sr + si * si
    squared = model * model
    fields = [
        ur * ur + ui * ui, model, squared * (east * east), squared * (east * north),
        squared * (north * north), chi_acc[...],
    ]
    lane = lax.broadcasted_iota(jnp.int32, (CH, LANES), 1)
    table = jnp.zeros((CH, LANES), f32)
    for place, field in enumerate(fields):
        table = jnp.where(lane == place, jnp.sum(field, axis=1, keepdims=True), table)
    square[CH:, :] = jnp.zeros((LANES - CH, LANES), f32)
    square[:CH, :] = table
    local = square[...].T[:8, :]

    channel = band * CH + lax.broadcasted_iota(jnp.int32, (1, LANES), 1)
    frequency = 1.0 + channel.astype(f32) * (1.0 / CHANNEL_COUNT)
    squares = frequency * frequency
    slope_parts = squares * local[2:5]
    at = lax.broadcasted_iota(jnp.int32, (1, N * LANES), 1)
    band_channel = (at // LANES) * CH + lax.rem(at, LANES)
    band_frequency = 1.0 + band_channel.astype(f32) * (1.0 / CHANNEL_COUNT)
    my_groups = vec_t[pl.ds(pl.multiple_of(band * OWN, OWN), OWN), :]

    loads[7].wait()
    arrivals(mod_sem.at[1], coef_buf.at[0:N - 1]).wait()
    arrivals(mod_sem.at[0], coef_buf.at[0:N - 1]).wait()
    weights_east = model_band[...] * my_groups[:, 0:1]
    weights_north = model_band[...] * my_groups[:, 1:2]

    arrivals(cr_sem.at[1], coef_buf.at[0:N - 1]).wait()
    coef = coef_buf[0]
    for source in range(1, N):
        coef = coef + coef_buf[source]
    coef = two_parts(coef)
    phases = joined(dot(jnp.concatenate([coef, coef], axis=1), back[...]))
    right_east = jnp.sum(weights_east * phases, axis=0, keepdims=True)
    right_north = jnp.sum(weights_north * phases, axis=0, keepdims=True)
    slope_east = jnp.sum(band_frequency * right_east, axis=1, keepdims=True)
    slope_north = jnp.sum(band_frequency * right_north, axis=1, keepdims=True)
    first_lane = lax.broadcasted_iota(jnp.int32, (1, LANES), 1) == 0
    slope_rows = jnp.concatenate(
        [jnp.where(first_lane, slope_east, 0.0), jnp.where(first_lane, slope_north, 0.0),
         slope_parts, jnp.zeros((1, LANES), f32)], axis=0)
    for other in range(N):
        lanes = slice(other * LANES, (other + 1) * LANES)
        band_send_buf[other] = jnp.concatenate([right_east[:, lanes], right_north[:, lanes], slope_rows], axis=0)

    def band_copy(source, other):
        return pltpu.make_async_remote_copy(
            src_ref=band_send_buf.at[other], dst_ref=band_buf.at[source],
            send_sem=band_sem.at[0], recv_sem=band_sem.at[1],
            device_id=(me, other), device_id_type=MESH)

    others(lambda r: band_copy(band, chan_other(r)).start())
    band_buf[band] = band_send_buf[band]
    arrivals(cr_sem.at[0], coef_buf.at[0:N - 1]).wait()
    arrivals(band_sem.at[1], coef_buf.at[0:N - 1]).wait()
    sums = band_buf[0]
    for source in range(1, N):
        sums = sums + band_buf[source]

    tot_buf[me] = jnp.concatenate(
        [local[0:5], sums[0:2], local[5:6], sums[2:7], jnp.zeros((3, LANES), f32)], axis=0)

    def tot_copy(source, other):
        return pltpu.make_async_remote_copy(
            src_ref=tot_buf.at[source], dst_ref=tot_buf.at[source],
            send_sem=tot_sem.at[0], recv_sem=tot_sem.at[1],
            device_id=(other, band), device_id_type=MESH)

    others(lambda r: tot_copy(me, grp_other(r)).start())
    arrivals(band_sem.at[0], coef_buf.at[0:N - 1]).wait()
    arrivals(tot_sem.at[1], tot_buf.at[0:N - 1]).wait()
    totals = tot_buf[0]
    for source in range(1, N):
        totals = totals + tot_buf[source]
    arrivals(tot_sem.at[0], tot_buf.at[0:N - 1]).wait()
    chi_out[...] = totals[7:8, :CH]

    terms = jnp.sum(totals[8:16], axis=1, keepdims=True)
    slope_east, slope_north = solve_pair(
        terms[2:3], terms[3:4], terms[4:5], terms[0:1], terms[1:2])
    tilt_east, tilt_north = solve_pair(
        totals[2:3], totals[3:4], totals[4:5], totals[5:6], totals[6:7])
    tilt_east = tilt_east - frequency * slope_east
    tilt_north = tilt_north - frequency * slope_north
    amplitude = jnp.sqrt((totals[0:1] + EPSILON) / (totals[1:2] + EPSILON))
    square[0:8, :] = jnp.concatenate(
        [frequency, tilt_east, tilt_north, 1.0 / amplitude, jnp.zeros((4, LANES), f32)], axis=0)
    columns = square[...].T[:CH, :]
    along = slope_east * east + slope_north * north
    turn = columns[:, 0:1] * along + columns[:, 1:2] * east + columns[:, 2:3] * north
    rotation_cos = jnp.cos(turn) * columns[:, 3:4]
    rotation_sin = jnp.sin(turn) * columns[:, 3:4]
    cal_out[0] = ur * rotation_cos + ui * rotation_sin
    cal_out[1] = ui * rotation_cos - ur * rotation_sin


def store(gains, cal, chi, gains_out, cal_out, chi_out, sem):
    copies = [
        pltpu.make_async_copy(source, target, sem.at[place])
        for place, (source, target) in enumerate(((gains, gains_out), (cal, cal_out), (chi, chi_out)))
    ]
    for copy in copies:
        copy.start()
    for copy in copies:
        copy.wait()


def per_device(ahead, back, vis, ants, gid, sky, start, coords):
    vmem = pl.BlockSpec(memory_space=pltpu.VMEM)
    hbm = pl.BlockSpec(memory_space=pltpu.HBM)
    dma = pltpu.SemaphoreType.DMA
    gains, cal, chi = pl.pallas_call(
        kernel,
        out_shape=(
            jax.ShapeDtypeStruct((2, CH, ANT), f32),
            jax.ShapeDtypeStruct((2, CH, GRP), f32),
            jax.ShapeDtypeStruct((1, CH), f32),
        ),
        in_specs=[hbm] * 8,
        out_specs=(vmem, vmem, vmem),
        scratch_shapes=[
            pltpu.VMEM((2, CH, BL), f32),
            pltpu.VMEM((2, BL), jnp.int32),
            pltpu.VMEM((1, BL), jnp.int32),
            pltpu.VMEM((2, CH, GRP), f32),
            pltpu.VMEM((2, CH, ANT), f32),
            pltpu.VMEM((2, ANT), f32),
            pltpu.VMEM((4 * NDLY, 4 * CH), bf16),
            pltpu.VMEM((4 * NDLY, N * LANES), bf16),
            pltpu.VMEM((STEPS, ANT_PAD, 2 * TILE), bf16),
            pltpu.VMEM((STEPS, GRP, TILE), bf16),
            pltpu.VMEM((2 * BL, ANT_PAD), bf16),
            pltpu.VMEM((BL, GRP), bf16),
            pltpu.VMEM((6 * CHK, BL), bf16),
            pltpu.VMEM((6 * CHK, 2 * BL), bf16),
            pltpu.VMEM((STEPS, 2 * CHK, 2 * TILE), f32),
            pltpu.VMEM((CHUNKS, UNITS, 2, 8, LANES), f32),
            pltpu.VMEM((2, CH, ANT_PAD), f32),
            pltpu.VMEM((4 * CHK, ANT_PAD), bf16),
            pltpu.VMEM((6 * CHK, GRP), f32),
            pltpu.VMEM((2, CH, GRP), f32),
            pltpu.VMEM((4 * CHK, GRP), bf16),
            pltpu.VMEM((6 * CHK, ANT_PAD), f32),
            pltpu.VMEM((CHUNKS, UNITS, 3, 8, LANES), f32),
            pltpu.VMEM((CHUNKS, N, 3, 8, LANES), f32),
            pltpu.VMEM((2 * CH, GRP), f32),
            pltpu.VMEM((GRP, 2 * NDLY), f32),
            pltpu.VMEM((N, OWN, 2 * NDLY), f32),
            pltpu.VMEM((GRP, LANES), f32),
            pltpu.VMEM((OWN, N * LANES), f32),
            pltpu.VMEM((LANES, LANES), f32),
            pltpu.VMEM((8, GRP), f32),
            pltpu.VMEM((GRP, LANES), f32),
            pltpu.VMEM((CH, LANES), f32),
            pltpu.VMEM((N, 8, LANES), f32),
            pltpu.VMEM((N, 8, LANES), f32),
            pltpu.VMEM((N, 16, LANES), f32),
            dma((7 + CHUNKS,)),
            dma((CHUNKS,)), dma((CHUNKS,)), dma((CHUNKS,)), dma((CHUNKS,)),
        ] + [dma((2,))] * 4,
        compiler_params=pltpu.CompilerParams(
            collective_id=0, has_side_effects=True, vmem_limit_bytes=60 * 1024 * 1024),
        cost_estimate=pl.CostEstimate(flops=20_000_000_000, bytes_accessed=4_000_000, transcendentals=0),
    )(vis, ants, gid, sky, start, coords, ahead, back)
    gains, cal, chi = pl.pallas_call(
        store,
        out_shape=(
            jax.ShapeDtypeStruct((2, CH, ANT), f32),
            jax.ShapeDtypeStruct((2, CH, GRP), f32),
            jax.ShapeDtypeStruct((1, CH), f32),
        ),
        in_specs=[vmem] * 3,
        out_specs=(hbm, hbm, hbm),
        scratch_shapes=[dma((3,))],
    )(gains, cal, chi)
    return gains, cal, chi.reshape(CH)


def solution(mesh):
    ahead, back = delay_tables()

    def program(vis, ants, gid, sky, start, coords):
        return jax.shard_map(
            functools.partial(per_device, ahead, back),
            mesh=mesh,
            in_specs=(
                P(None, "chan", "grp"),
                P(None, "grp"),
                P("grp", None),
                P(None, "chan", "grp"),
                P(None, "chan", None),
                P(),
            ),
            out_specs=(P(None, "chan", None), P(None, "chan", "grp"), P("chan")),
            check_vma=False,
        )(vis, ants, gid, sky, start, coords)

    return program
```

```python
import functools

import jax
import jax.numpy as jnp
import numpy as np
from jax import lax
from jax.experimental import pallas as pl
from jax.experimental.pallas import tpu as pltpu
from jax.sharding import PartitionSpec as P

CHANNEL_COUNT = 1536
NDLY = 64
ITERS = 4
RIDGE = 0.5
EPSILON = 1e-06

N = 16
ANT = 350
ANT_PAD = 384
CH = 96
CHUNKS = 3
CHK = CH // CHUNKS
BL = 2048
GRP = 128
TILE = 256
STEPS = BL // TILE
SPAN = 8
OWN = GRP // N
LANES = 128
UNITS = (CHK // 8) * (ANT_PAD // LANES)

GRP_STEPS = sorted(
    ((dx, dy) for dx in range(4) for dy in range(4) if dx or dy),
    key=lambda step: -min(step[0], 4 - step[0]) - min(step[1], 4 - step[1]))
CHAN_STEPS = sorted(
    ((dz, core) for dz in range(8) for core in range(2) if dz or core),
    key=lambda step: -2 * min(step[0], 8 - step[0]) - step[1])

ACROSS = ANT_PAD // LANES

MESH = pl.DeviceIdType.MESH
f32 = jnp.float32
bf16 = jnp.bfloat16


def owner_of(unit):
    return unit + 1 + unit // 4


def two_parts(number):
    first = number.astype(bf16)
    rest = (number - first.astype(f32)).astype(bf16)
    return jnp.concatenate([first, rest], axis=0)


def joined(parts):
    half = parts.shape[0] // 2
    return parts[:half] + parts[half:]


def dot(left, right):
    return jnp.dot(left, right, preferred_element_type=f32)


def dot_last(left, right):
    return lax.dot_general(left, right, (((1,), (1,)), ((), ())), preferred_element_type=f32)


def solve_pair(entry_xx, entry_xy, entry_yy, right_x, right_y):
    ridge_shift = 0.001 * (entry_xx + entry_yy) + EPSILON
    diag_first = entry_xx + ridge_shift
    diag_second = entry_yy + ridge_shift
    determinant = diag_first * diag_second - entry_xy * entry_xy
    return (
        (diag_second * right_x - entry_xy * right_y) / determinant,
        (diag_first * right_y - entry_xy * right_x) / determinant,
    )


def delay_tables():
    channel_ids = np.arange(CHANNEL_COUNT)
    turns = (channel_ids[:, None] * (np.arange(NDLY)[None, :] - NDLY // 2)) % CHANNEL_COUNT
    angles = 2.0 * np.pi / CHANNEL_COUNT * turns
    cosines = np.cos(angles).reshape(N, CH, NDLY).transpose(0, 2, 1)
    sines = np.sin(angles).reshape(N, CH, NDLY).transpose(0, 2, 1)
    ahead = np.concatenate(
        [np.concatenate([cosines, sines], axis=2), np.concatenate([-sines, cosines], axis=2)], axis=1
    )
    back = np.zeros((2 * NDLY, N, LANES))
    back[:NDLY, :, :CH] = sines.transpose(1, 0, 2)
    back[NDLY:, :, :CH] = cosines.transpose(1, 0, 2)
    ahead = ahead / CHANNEL_COUNT
    back = back.reshape(2 * NDLY, N * LANES)
    ahead_1, back_1 = ahead.astype(bf16), back.astype(bf16)
    ahead_2 = (ahead - ahead_1.astype(np.float64)).astype(bf16)
    back_2 = (back - back_1.astype(np.float64)).astype(bf16)
    ahead = np.concatenate(
        [np.concatenate([ahead_1, ahead_1], axis=2), np.concatenate([ahead_2, ahead_2], axis=2)], axis=1)
    return ahead, np.concatenate([back_1, back_2], axis=0)


def kernel(
    vis_hbm, ants_hbm, gid_hbm, sky_hbm, start_hbm, coords_hbm, ahead_hbm, back_hbm,
    gains_out, cal_out, chi_out,
    vis, ants, gid, sky, start, coords, ahead, back,
    hot, grp_hot, hot_t, grp_hot_t, rows_a, rows_b, pair, gain, wide, gain2, acc_grp, unique, unique2, acc_sum, acc_ant, rs_buf,
    ratio, part, coef_buf, model_t, model_band, square, vec_acc, vec_t, chi_acc,
    band_send_buf, band_buf, tot_buf,
    load_sem, rs_send, rs_recv, ag_send, ag_recv, mod_sem, cr_sem, band_sem, tot_sem,
):
    me = lax.axis_index("grp")
    band = lax.axis_index("chan")
    i_own = lax.rem(me, 5) != 0
    my_unit = me - 1 - me // 5

    def others(body):
        for r in range(1, N):
            body(r)

    def grp_other(r):
        dx, dy = GRP_STEPS[r - 1]
        x = me // 4
        return lax.rem(x + dx, 4) * 4 + lax.rem(me - 4 * x + dy, 4)

    def chan_other(r):
        dz, core = CHAN_STEPS[r - 1]
        z = band // 2
        return lax.rem(z + dz, 8) * 2 + lax.rem(band - 2 * z + core, 2)

    loads = [
        pltpu.make_async_copy(ants_hbm, ants, load_sem.at[0]),
        pltpu.make_async_copy(gid_hbm, gid, load_sem.at[1]),
        pltpu.make_async_copy(coords_hbm, coords, load_sem.at[2]),
        pltpu.make_async_copy(start_hbm, start, load_sem.at[3]),
        pltpu.make_async_copy(vis_hbm.at[:, 0:CHK], vis.at[:, 0:CHK], load_sem.at[4]),
        pltpu.make_async_copy(sky_hbm, sky, load_sem.at[5]),
        pltpu.make_async_copy(ahead_hbm.at[band], ahead, load_sem.at[6]),
        pltpu.make_async_copy(back_hbm, back, load_sem.at[7]),
    ] + [
        pltpu.make_async_copy(
            vis_hbm.at[:, c * CHK:(c + 1) * CHK], vis.at[:, c * CHK:(c + 1) * CHK], load_sem.at[7 + c])
        for c in range(1, CHUNKS)
    ]
    for load in loads:
        load.start()

    barrier = pltpu.get_barrier_semaphore()

    def greet(r):
        pl.semaphore_signal(barrier, inc=1, device_id=(grp_other(r), band), device_id_type=MESH)
        pl.semaphore_signal(barrier, inc=1, device_id=(me, chan_other(r)), device_id_type=MESH)

    others(greet)

    vec_acc[...] = jnp.zeros_like(vec_acc)
    wide[:, :, ANT_PAD - LANES:] = jnp.zeros((2, CH, LANES), f32)
    wide[0, :8, :] = jnp.zeros((8, ANT_PAD), f32)
    loads[0].wait()
    loads[1].wait()
    loads[2].wait()
    wide[0, 0:2, :ANT] = coords[...]
    places = two_parts(wide[0, :8, :])

    def build(t, carry):
        cols = pl.ds(pl.multiple_of(t * TILE, TILE), TILE)
        ant_ids = lax.broadcasted_iota(jnp.int32, (ANT_PAD, TILE), 0)
        grp_ids = lax.broadcasted_iota(jnp.int32, (GRP, TILE), 0)
        p_hot = jnp.where(ant_ids == ants[0:1, cols], 1.0, 0.0).astype(bf16)
        q_hot = jnp.where(ant_ids == ants[1:2, cols], 1.0, 0.0).astype(bf16)
        g_hot = jnp.where(grp_ids == gid[0:1, cols], 1.0, 0.0).astype(bf16)
        hot[t, :, :TILE] = p_hot
        hot[t, :, TILE:] = q_hot
        grp_hot[t] = g_hot
        here = pl.multiple_of(2 * t * TILE, TILE)
        hot_t[pl.ds(here, TILE), :] = p_hot.T
        hot_t[pl.ds(here + TILE, TILE), :] = q_hot.T
        grp_hot_t[cols, :] = g_hot.T
        place = joined(dot(places, p_hot - q_hot))
        row = lax.broadcasted_iota(jnp.int32, place.shape, 0)
        place = jnp.where(row == 2, 1.0, place)
        vec_acc[...] += joined(dot_last(two_parts(place), g_hot))
        return carry

    lax.fori_loop(0, STEPS, build, 0, unroll=STEPS)

    loads[3].wait()
    wide[:, :, :ANT] = start[...]
    for chunk in range(CHUNKS):
        for unit in range(UNITS):
            row, lane = chunk * CHK + unit // ACROSS * 8, unit % ACROSS * LANES
            gain[chunk, unit] = wide[:, row:row + 8, lane:lane + LANES]
    loads[4].wait()

    def rows_of(chunk):
        return pl.ds(pl.multiple_of(chunk * CHK, CHK), CHK)

    def group_fit(chunk):
        mine = rows_of(chunk)
        gain2[...] = two_parts(jnp.concatenate(
            [jnp.concatenate([gain[chunk, tile * ACROSS + l, q] for l in range(ACROSS)], axis=1)
             for q in range(2) for tile in range(CHK // 8)], axis=0))

        for t in range(STEPS):
            cols = slice(t * TILE, (t + 1) * TILE)
            pq = joined(dot(gain2[...], hot[t]))
            pair[t] = pq
            a, b = pq[:CHK, :TILE], pq[CHK:, :TILE]
            c, d = pq[:CHK, TILE:], pq[CHK:, TILE:]
            x, y = vis[0, mine, cols], vis[1, mine, cols]
            wr = a * c + b * d
            wi = b * c - a * d
            rows = jnp.concatenate([x * wr + y * wi, y * wr - x * wi, wr * wr + wi * wi], axis=0)
            rows_a[:, cols] = two_parts(rows)
            if (t + 1) % SPAN == 0:
                part_cols = slice((t + 1 - SPAN) * TILE, (t + 1) * TILE)
                acc_grp[...] = dot(rows_a[:, part_cols], grp_hot_t[part_cols, :])

        sums = joined(acc_grp[...])
        scale = 1.0 / (sums[2 * CHK:] + RIDGE)
        ur, ui = sums[:CHK] * scale, sums[CHK:2 * CHK] * scale
        unique[0, mine, :] = ur
        unique[1, mine, :] = ui
        unique2[...] = two_parts(jnp.concatenate([ur, ui], axis=0))

    def antenna_sums(chunk):
        mine = rows_of(chunk)

        for t in range(STEPS):
            cols = slice(t * TILE, (t + 1) * TILE)
            uu = joined(dot(unique2[...], grp_hot[t]))
            s, v = uu[:CHK], uu[CHK:]
            pq = pair[t]
            a, b = pq[:CHK, :TILE], pq[CHK:, :TILE]
            c, d = pq[:CHK, TILE:], pq[CHK:, TILE:]
            x, y = vis[0, mine, cols], vis[1, mine, cols]
            zr = s * x + v * y
            zi = s * y - v * x
            size = s * s + v * v
            for_p = jnp.concatenate([c * zr - d * zi, c * zi + d * zr, size * (c * c + d * d)], axis=0)
            for_q = jnp.concatenate([a * zr + b * zi, b * zr - a * zi, size * (a * a + b * b)], axis=0)
            rows_b[:, 2 * t * TILE:(2 * t + 1) * TILE] = two_parts(for_p)
            rows_b[:, (2 * t + 1) * TILE:(2 * t + 2) * TILE] = two_parts(for_q)
            if (t + 1) % SPAN == 0:
                part_cols = slice(2 * (t + 1 - SPAN) * TILE, 2 * (t + 1) * TILE)
                acc_sum[...] = dot(rows_b[:, part_cols], hot_t[part_cols, :])

        sums = joined(acc_sum[...]).reshape(3, CHK, ANT_PAD)
        for unit in range(UNITS):
            row, lane = unit // ACROSS * 8, unit % ACROSS * LANES
            acc_ant[chunk, unit] = sums[:, row:row + 8, lane:lane + LANES]

    def misfit(chunk):
        mine = rows_of(chunk)
        chi_acc[mine, :] = jnp.zeros((CHK, LANES), f32)

        def step(t, carry):
            cols = pl.ds(pl.multiple_of(t * TILE, TILE), TILE)
            uu = joined(dot(unique2[...], grp_hot[t]))
            s, v = uu[:CHK], uu[CHK:]
            pq = pair[t]
            a, b = pq[:CHK, :TILE], pq[CHK:, :TILE]
            c, d = pq[:CHK, TILE:], pq[CHK:, TILE:]
            wr = a * c + b * d
            wi = b * c - a * d
            er = vis[0, mine, cols] - (wr * s - wi * v)
            ei = vis[1, mine, cols] - (wr * v + wi * s)
            e = er * er + ei * ei
            chi_acc[mine, :] += e[:, :LANES] + e[:, LANES:]
            return carry

        lax.fori_loop(0, STEPS, step, 0, unroll=STEPS)

    def rs_copy(chunk, unit):
        return pltpu.make_async_remote_copy(
            src_ref=acc_ant.at[chunk, unit],
            dst_ref=rs_buf.at[chunk, me],
            send_sem=rs_send.at[chunk], recv_sem=rs_recv.at[chunk],
            device_id=(owner_of(unit), band), device_id_type=MESH)

    def arrivals(sem, shape):
        return pltpu.make_async_copy(shape, shape, sem)

    def ag_copy(chunk, unit, other):
        return pltpu.make_async_remote_copy(
            src_ref=gain.at[chunk, unit], dst_ref=gain.at[chunk, unit],
            send_sem=ag_send.at[chunk], recv_sem=ag_recv.at[chunk],
            device_id=(other, band), device_id_type=MESH)

    def units(body):
        def one(r):
            other = grp_other(r)

            @pl.when(lax.rem(other, 5) != 0)
            def _():
                body(other - 1 - other // 5)

        others(one)

    def send_sums(chunk):
        units(lambda unit: rs_copy(chunk, unit).start())

    def update_gains(chunk):
        @pl.when(i_own)
        def _():
            rs_buf[chunk, me] = acc_ant[chunk, my_unit]
            arrivals(rs_recv.at[chunk], rs_buf.at[chunk, 0:N - 1]).wait()
            total = rs_buf[chunk, 0]
            for source in range(1, N):
                total = total + rs_buf[chunk, source]
            share = 0.5 / (total[2] + RIDGE)
            gain[chunk, my_unit] = 0.5 * gain[chunk, my_unit] + total[:2] * share
            others(lambda r: ag_copy(chunk, my_unit, grp_other(r)).start())

    def by_place(body):
        @pl.when(i_own)
        def _():
            body(UNITS - 1)

        @pl.when(jnp.logical_not(i_own))
        def _():
            body(UNITS)

    def await_gains(chunk):
        by_place(lambda n: arrivals(ag_recv.at[chunk], rs_buf.at[chunk, 0:n, 0:2]).wait())

    def settle(chunk):
        by_place(lambda n: arrivals(rs_send.at[chunk], rs_buf.at[chunk, 0:n]).wait())

        @pl.when(i_own)
        def _():
            arrivals(ag_send.at[chunk], rs_buf.at[chunk, 0:N - 1, 0:2]).wait()

    def mod_copy(source, other):
        return pltpu.make_async_remote_copy(
            src_ref=model_t.at[pl.ds(pl.multiple_of(other * OWN, OWN), OWN), :],
            dst_ref=model_band.at[:, pl.ds(pl.multiple_of(source * LANES, LANES), LANES)],
            send_sem=mod_sem.at[0], recv_sem=mod_sem.at[1],
            device_id=(me, other), device_id_type=MESH)

    def iteration(s, carry):
        chunk = lax.rem(s, CHUNKS)

        @pl.when(s >= CHUNKS)
        def _():
            await_gains(chunk)

        for c in range(1, CHUNKS):
            @pl.when(s == c)
            def _():
                loads[7 + c].wait()

        group_fit(chunk)

        @pl.when(s >= CHUNKS)
        def _():
            settle(chunk)

        antenna_sums(chunk)

        @pl.when(s == 0)
        def _():
            pl.semaphore_wait(barrier, 2 * (N - 1))

        send_sums(chunk)

        @pl.when(s == CHUNKS - 1)
        def _():
            loads[5].wait()
            model = sky[0] * sky[0] + sky[1] * sky[1]
            square[CH:, :] = jnp.zeros((LANES - CH, LANES), f32)
            square[:CH, :] = model
            model_t[...] = square[...].T
            own_rows = pl.ds(pl.multiple_of(band * OWN, OWN), OWN)
            own_lanes = pl.ds(pl.multiple_of(band * LANES, LANES), LANES)
            model_band[:, own_lanes] = model_t[own_rows, :]
            others(lambda r: mod_copy(band, chan_other(r)).start())

        final = ITERS * CHUNKS - 1

        @pl.when(jnp.logical_and(s >= 1, s <= final - CHUNKS + 1))
        def _():
            update_gains(lax.rem(s + CHUNKS - 1, CHUNKS))

        @pl.when(s == final)
        def _():
            def each(c, carry):
                update_gains(c)
                return carry

            lax.fori_loop(0, CHUNKS, each, 0)

        return carry

    lax.fori_loop(0, ITERS * CHUNKS, iteration, 0)

    def last(chunk, carry):
        await_gains(chunk)
        group_fit(chunk)

        settle(chunk)

        @pl.when(chunk < CHUNKS - 1)
        def _():
            misfit(chunk)

        return carry

    lax.fori_loop(0, CHUNKS, last, 0)

    ur, ui = unique[0], unique[1]
    sr, si = sky[0], sky[1]
    ratio[:CH, :] = ur * sr + ui * si
    ratio[CH:, :] = ui * sr - ur * si
    loads[6].wait()
    part[...] = joined(dot(ahead[...], two_parts(ratio[...]))).T

    def cr_copy(source, other):
        return pltpu.make_async_remote_copy(
            src_ref=part.at[pl.ds(pl.multiple_of(other * OWN, OWN), OWN), :], dst_ref=coef_buf.at[source],
            send_sem=cr_sem.at[0], recv_sem=cr_sem.at[1],
            device_id=(me, other), device_id_type=MESH)

    others(lambda r: cr_copy(band, chan_other(r)).start())
    coef_buf[band] = part[pl.ds(pl.multiple_of(band * OWN, OWN), OWN), :]
    misfit(CHUNKS - 1)

    for chunk in range(CHUNKS):
        for unit in range(UNITS):
            row, lane = chunk * CHK + unit // ACROSS * 8, unit % ACROSS * LANES
            wide[:, row:row + 8, lane:lane + LANES] = gain[chunk, unit]
    start[...] = wide[:, :, :ANT]
    copy_gains = pltpu.make_async_copy(start, gains_out, load_sem.at[7 + CHUNKS])
    copy_gains.start()
    east = vec_acc[0:1, :] / vec_acc[2:3, :]
    north = vec_acc[1:2, :] / vec_acc[2:3, :]
    square[...] = jnp.zeros_like(square)
    square[0:1, :] = east
    square[1:2, :] = north
    vec_t[...] = square[...].T
    model = sr * sr + si * si
    squared = model * model
    fields = [
        ur * ur + ui * ui, model, squared * (east * east), squared * (east * north),
        squared * (north * north), chi_acc[...],
    ]
    lane = lax.broadcasted_iota(jnp.int32, (CH, LANES), 1)
    table = jnp.zeros((CH, LANES), f32)
    for place, field in enumerate(fields):
        table = jnp.where(lane == place, jnp.sum(field, axis=1, keepdims=True), table)
    square[CH:, :] = jnp.zeros((LANES - CH, LANES), f32)
    square[:CH, :] = table
    local = square[...].T[:8, :]

    channel = band * CH + lax.broadcasted_iota(jnp.int32, (1, LANES), 1)
    frequency = 1.0 + channel.astype(f32) * (1.0 / CHANNEL_COUNT)
    squares = frequency * frequency
    slope_parts = squares * local[2:5]
    at = lax.broadcasted_iota(jnp.int32, (1, N * LANES), 1)
    band_channel = (at // LANES) * CH + lax.rem(at, LANES)
    band_frequency = 1.0 + band_channel.astype(f32) * (1.0 / CHANNEL_COUNT)
    my_groups = vec_t[pl.ds(pl.multiple_of(band * OWN, OWN), OWN), :]

    loads[7].wait()
    arrivals(mod_sem.at[1], coef_buf.at[0:N - 1]).wait()
    arrivals(mod_sem.at[0], coef_buf.at[0:N - 1]).wait()
    weights_east = model_band[...] * my_groups[:, 0:1]
    weights_north = model_band[...] * my_groups[:, 1:2]

    arrivals(cr_sem.at[1], coef_buf.at[0:N - 1]).wait()
    coef = coef_buf[0]
    for source in range(1, N):
        coef = coef + coef_buf[source]
    coef = two_parts(coef)
    phases = joined(dot(jnp.concatenate([coef, coef], axis=1), back[...]))
    right_east = jnp.sum(weights_east * phases, axis=0, keepdims=True)
    right_north = jnp.sum(weights_north * phases, axis=0, keepdims=True)
    slope_east = jnp.sum(band_frequency * right_east, axis=1, keepdims=True)
    slope_north = jnp.sum(band_frequency * right_north, axis=1, keepdims=True)
    first_lane = lax.broadcasted_iota(jnp.int32, (1, LANES), 1) == 0
    slope_rows = jnp.concatenate(
        [jnp.where(first_lane, slope_east, 0.0), jnp.where(first_lane, slope_north, 0.0),
         slope_parts, jnp.zeros((1, LANES), f32)], axis=0)
    for other in range(N):
        lanes = slice(other * LANES, (other + 1) * LANES)
        band_send_buf[other] = jnp.concatenate([right_east[:, lanes], right_north[:, lanes], slope_rows], axis=0)

    def band_copy(source, other):
        return pltpu.make_async_remote_copy(
            src_ref=band_send_buf.at[other], dst_ref=band_buf.at[source],
            send_sem=band_sem.at[0], recv_sem=band_sem.at[1],
            device_id=(me, other), device_id_type=MESH)

    others(lambda r: band_copy(band, chan_other(r)).start())
    band_buf[band] = band_send_buf[band]
    arrivals(cr_sem.at[0], coef_buf.at[0:N - 1]).wait()
    arrivals(band_sem.at[1], coef_buf.at[0:N - 1]).wait()
    sums = band_buf[0]
    for source in range(1, N):
        sums = sums + band_buf[source]

    tot_buf[me] = jnp.concatenate(
        [local[0:5], sums[0:2], local[5:6], sums[2:7], jnp.zeros((3, LANES), f32)], axis=0)

    def tot_copy(source, other):
        return pltpu.make_async_remote_copy(
            src_ref=tot_buf.at[source], dst_ref=tot_buf.at[source],
            send_sem=tot_sem.at[0], recv_sem=tot_sem.at[1],
            device_id=(other, band), device_id_type=MESH)

    others(lambda r: tot_copy(me, grp_other(r)).start())
    arrivals(band_sem.at[0], coef_buf.at[0:N - 1]).wait()
    arrivals(tot_sem.at[1], tot_buf.at[0:N - 1]).wait()
    totals = tot_buf[0]
    for source in range(1, N):
        totals = totals + tot_buf[source]
    arrivals(tot_sem.at[0], tot_buf.at[0:N - 1]).wait()
    chi_out[...] = totals[7:8, :CH]

    terms = jnp.sum(totals[8:16], axis=1, keepdims=True)
    slope_east, slope_north = solve_pair(
        terms[2:3], terms[3:4], terms[4:5], terms[0:1], terms[1:2])
    tilt_east, tilt_north = solve_pair(
        totals[2:3], totals[3:4], totals[4:5], totals[5:6], totals[6:7])
    tilt_east = tilt_east - frequency * slope_east
    tilt_north = tilt_north - frequency * slope_north
    amplitude = jnp.sqrt((totals[0:1] + EPSILON) / (totals[1:2] + EPSILON))
    square[0:8, :] = jnp.concatenate(
        [frequency, tilt_east, tilt_north, 1.0 / amplitude, jnp.zeros((4, LANES), f32)], axis=0)
    columns = square[...].T[:CH, :]
    along = slope_east * east + slope_north * north
    turn = columns[:, 0:1] * along + columns[:, 1:2] * east + columns[:, 2:3] * north
    rotation_cos = jnp.cos(turn) * columns[:, 3:4]
    rotation_sin = jnp.sin(turn) * columns[:, 3:4]
    cal_out[0] = ur * rotation_cos + ui * rotation_sin
    cal_out[1] = ui * rotation_cos - ur * rotation_sin
    copy_gains.wait()


def store(gains, cal, chi, gains_out, cal_out, chi_out, sem):
    copies = [
        pltpu.make_async_copy(source, target, sem.at[place])
        for place, (source, target) in enumerate(((gains, gains_out), (cal, cal_out), (chi, chi_out)))
    ]
    for copy in copies:
        copy.start()
    for copy in copies:
        copy.wait()


def per_device(ahead, back, vis, ants, gid, sky, start, coords):
    vmem = pl.BlockSpec(memory_space=pltpu.VMEM)
    hbm = pl.BlockSpec(memory_space=pltpu.HBM)
    dma = pltpu.SemaphoreType.DMA
    gains, cal, chi = pl.pallas_call(
        kernel,
        out_shape=(
            jax.ShapeDtypeStruct((2, CH, ANT), f32),
            jax.ShapeDtypeStruct((2, CH, GRP), f32),
            jax.ShapeDtypeStruct((1, CH), f32),
        ),
        in_specs=[hbm] * 8,
        out_specs=(hbm, vmem, vmem),
        scratch_shapes=[
            pltpu.VMEM((2, CH, BL), f32),
            pltpu.VMEM((2, BL), jnp.int32),
            pltpu.VMEM((1, BL), jnp.int32),
            pltpu.VMEM((2, CH, GRP), f32),
            pltpu.VMEM((2, CH, ANT), f32),
            pltpu.VMEM((2, ANT), f32),
            pltpu.VMEM((4 * NDLY, 4 * CH), bf16),
            pltpu.VMEM((4 * NDLY, N * LANES), bf16),
            pltpu.VMEM((STEPS, ANT_PAD, 2 * TILE), bf16),
            pltpu.VMEM((STEPS, GRP, TILE), bf16),
            pltpu.VMEM((2 * BL, ANT_PAD), bf16),
            pltpu.VMEM((BL, GRP), bf16),
            pltpu.VMEM((6 * CHK, BL), bf16),
            pltpu.VMEM((6 * CHK, 2 * BL), bf16),
            pltpu.VMEM((STEPS, 2 * CHK, 2 * TILE), f32),
            pltpu.VMEM((CHUNKS, UNITS, 2, 8, LANES), f32),
            pltpu.VMEM((2, CH, ANT_PAD), f32),
            pltpu.VMEM((4 * CHK, ANT_PAD), bf16),
            pltpu.VMEM((6 * CHK, GRP), f32),
            pltpu.VMEM((2, CH, GRP), f32),
            pltpu.VMEM((4 * CHK, GRP), bf16),
            pltpu.VMEM((6 * CHK, ANT_PAD), f32),
            pltpu.VMEM((CHUNKS, UNITS, 3, 8, LANES), f32),
            pltpu.VMEM((CHUNKS, N, 3, 8, LANES), f32),
            pltpu.VMEM((2 * CH, GRP), f32),
            pltpu.VMEM((GRP, 2 * NDLY), f32),
            pltpu.VMEM((N, OWN, 2 * NDLY), f32),
            pltpu.VMEM((GRP, LANES), f32),
            pltpu.VMEM((OWN, N * LANES), f32),
            pltpu.VMEM((LANES, LANES), f32),
            pltpu.VMEM((8, GRP), f32),
            pltpu.VMEM((GRP, LANES), f32),
            pltpu.VMEM((CH, LANES), f32),
            pltpu.VMEM((N, 8, LANES), f32),
            pltpu.VMEM((N, 8, LANES), f32),
            pltpu.VMEM((N, 16, LANES), f32),
            dma((8 + CHUNKS,)),
            dma((CHUNKS,)), dma((CHUNKS,)), dma((CHUNKS,)), dma((CHUNKS,)),
        ] + [dma((2,))] * 4,
        compiler_params=pltpu.CompilerParams(
            collective_id=0, has_side_effects=True, vmem_limit_bytes=60 * 1024 * 1024),
        cost_estimate=pl.CostEstimate(flops=20_000_000_000, bytes_accessed=4_000_000, transcendentals=0),
    )(vis, ants, gid, sky, start, coords, ahead, back)
    gains, cal, chi = pl.pallas_call(
        store,
        out_shape=(
            jax.ShapeDtypeStruct((2, CH, ANT), f32),
            jax.ShapeDtypeStruct((2, CH, GRP), f32),
            jax.ShapeDtypeStruct((1, CH), f32),
        ),
        in_specs=[vmem] * 3,
        out_specs=(hbm, hbm, hbm),
        scratch_shapes=[dma((3,))],
    )(gains, cal, chi)
    return gains, cal, chi.reshape(CH)


def solution(mesh):
    ahead, back = delay_tables()

    def program(vis, ants, gid, sky, start, coords):
        return jax.shard_map(
            functools.partial(per_device, ahead, back),
            mesh=mesh,
            in_specs=(
                P(None, "chan", "grp"),
                P(None, "grp"),
                P("grp", None),
                P(None, "chan", "grp"),
                P(None, "chan", None),
                P(),
            ),
            out_specs=(P(None, "chan", None), P(None, "chan", "grp"), P("chan")),
            check_vma=False,
        )(vis, ants, gid, sky, start, coords)

    return program
```
